32 devices in a mesh: groups: 2 (over y), row: 4 (over z), col: 2 (over x), chan: 2 (over core).
Axes of the slice: x: 2, y: 2, z: 4, core: 2. Of those that a mesh axis runs over, the one named last changes fastest.
Arguments:
- pair_input: bfloat16 [512, 256, 128], P(('groups', 'row'), ('col', 'chan')), parts along dimension 0, may hold values from -6 to 6
- alignment_features: bfloat16 [128, 512, 64], P('row', ('groups', 'col', 'chan')), parts along dimension 1, may hold values from -6 to 6
- alignment_mask: int32 [128, 512], P('row', ('groups', 'col', 'chan')), parts along dimension 1, may hold values from 0 to 1
- token_valid: int32 [512], P('groups'), parts along dimension 0, may hold values from 0 to 1, as said below
- left_weight: bfloat16 [64, 32], replicated, may hold values from -0.75 to 0.75
- right_weight: bfloat16 [64, 32], replicated, may hold values from -0.75 to 0.75
- output_weight: bfloat16 [1024, 128], replicated, may hold values from -1.75 to 1.75
- gate_weight: bfloat16 [128, 512], replicated, may hold values from -0.5 to 0.5
- up_weight: bfloat16 [128, 512], replicated, may hold values from -0.5 to 0.5
- down_weight: bfloat16 [512, 128], replicated, may hold values from -0.25 to 0.25
- kernel_weight: bfloat16 [3, 3, 128, 128], replicated, may hold values from -0.1875 to 0.1875
Outputs:
- pair_out: bfloat16 [512, 256, 128], P(('groups', 'row'), ('col', 'chan')), parts along dimension 0
The draws below stay inside these ranges and needn't reach their ends.
There are 2 independent parts, one for each index of `groups`. The reference program is written for one: setup_inputs(seed, part) draws one part's arguments, and reference() takes and returns one part's arrays. A program takes and returns all parts, laid end to end along the dimension named above; an argument that names none is the same for every part. Nothing has to cross between parts.
Inputs may be any that keep to these rules, and one draw needn't show every extreme that they name: `token_valid`: the ones come first.
All inputs are finite; a program needn't handle non-finite values.
Results may differ from the reference program's by a relative error of at most 0.014.
Values may be sent and summed in bfloat16 or wider, within the bound.
No kernel may reach another device: no remote copies, remote signals or barrier semaphores. Data moves between devices by JAX's collectives and lax.ppermute only.
A program may use at most 64 MiB of HBM per device.

```python
import jax
import jax.numpy as jnp
from jax import lax

CPAIR = 128
ALIGN_CHANNELS = 64
COPM = 32
CHID = 512
TOKEN_COUNT = 256
ALIGN_ROWS = 128


def draw_alignment_mask(key, part):
    key_cover, key_vacant, key_keep = jax.random.split(jax.random.fold_in(key, 101), 3)
    coverage = jax.random.randint(key_cover, (TOKEN_COUNT,), ALIGN_ROWS // 2, ALIGN_ROWS + 1)
    vacant = jax.random.randint(key_vacant, (TOKEN_COUNT,), 0, 64)
    coverage = jnp.where(vacant == 0, 0, coverage)
    retained = jax.random.randint(key_keep, (ALIGN_ROWS, TOKEN_COUNT), 0, 8)
    seq_rows = jnp.arange(ALIGN_ROWS)[:, None]
    return ((seq_rows < coverage[None, :]) & (retained > 0)).astype(jnp.int32)


def draw_token_valid(key, part):
    length_key = jax.random.fold_in(key, 202)
    filled = jax.random.randint(length_key, (), TOKEN_COUNT - TOKEN_COUNT // 8, TOKEN_COUNT + 1)
    return (jnp.arange(TOKEN_COUNT) < filled).astype(jnp.int32)


def shard_levels(own_key, shape, cuts, low, largest):
    factor_of, own = 1.0, jax.random.fold_in(own_key, 6)
    for axis_at, shards_of in cuts:
        heights = jnp.exp(jax.random.uniform(jax.random.fold_in(own, axis_at), (shards_of,), jnp.float32, low / len(cuts), largest / len(cuts)))
        factor_of = factor_of * jnp.repeat(heights, shape[axis_at] // shards_of).reshape([-1 if axis == axis_at else 1 for axis in range(len(shape))])
    return factor_of


def bell_draw(stream_key, shape, deviation, reach, cuts=(), held_as=jnp.bfloat16):
    values = deviation * jax.random.normal(stream_key, shape, jnp.float32)
    if cuts:
        values = values * shard_levels(stream_key, shape, cuts, -0.22, 0.18)
    return jnp.clip(values, -reach, reach).astype(held_as)


def setup_inputs(seed: int = 0, part: int = 0) -> dict:
    splits = jax.random.split(jax.random.key(seed), 12)
    part_splits = jax.random.split(jax.random.fold_in(splits[11], part), 12)
    pair_input = bell_draw(part_splits[0], (TOKEN_COUNT, TOKEN_COUNT, CPAIR), 1.0, 6.0, ((0, 4), (1, 4)))
    alignment_features = bell_draw(part_splits[1], (ALIGN_ROWS, TOKEN_COUNT, ALIGN_CHANNELS), 1.0, 6.0, ((0, 4), (1, 4)))
    alignment_mask = draw_alignment_mask(jax.random.fold_in(jax.random.fold_in(splits[11], part), 71), part)
    token_valid = draw_token_valid(jax.random.fold_in(jax.random.fold_in(splits[11], part), 71), part)
    left_weight = bell_draw(splits[4], (ALIGN_CHANNELS, COPM), ALIGN_CHANNELS ** -0.5, 0.75)
    right_weight = bell_draw(splits[5], (ALIGN_CHANNELS, COPM), ALIGN_CHANNELS ** -0.5, 0.75)
    output_weight = bell_draw(splits[6], (COPM * COPM, CPAIR), 0.3, 1.75)
    gate_weight = bell_draw(splits[7], (CPAIR, CHID), CPAIR ** -0.5, 0.5)
    up_weight = bell_draw(splits[8], (CPAIR, CHID), CPAIR ** -0.5, 0.5)
    down_weight = bell_draw(splits[9], (CHID, CPAIR), CHID ** -0.5, 0.25)
    kernel_weight = bell_draw(splits[10], (3, 3, CPAIR, CPAIR), (9 * CPAIR) ** -0.5, 0.1875)
    return {"pair_input": pair_input, "alignment_features": alignment_features, "alignment_mask": alignment_mask, "token_valid": token_valid, "left_weight": left_weight, "right_weight": right_weight, "output_weight": output_weight, "gate_weight": gate_weight, "up_weight": up_weight, "down_weight": down_weight, "kernel_weight": kernel_weight}


epsilon = 1e-05
strip_rows = 16
slab_rows = 4096

def transition(pair_rows, gate_weight, up_weight, down_weight):
    values = pair_rows.astype(jnp.float32)
    centre = lax.optimization_barrier(jnp.mean(values, axis=-1, keepdims=True))
    spread = lax.optimization_barrier(jnp.mean(jnp.square(values - centre), axis=-1, keepdims=True))
    normed = ((values - centre) * lax.rsqrt(spread + epsilon)).astype(jnp.bfloat16)
    gate_act = jnp.dot(normed, gate_weight, preferred_element_type=jnp.float32)
    up_act = jnp.dot(normed, up_weight, preferred_element_type=jnp.float32)
    hidden = (jax.nn.silu(gate_act) * up_act).astype(jnp.bfloat16)
    return (values + jnp.dot(hidden, down_weight, preferred_element_type=jnp.float32)).astype(jnp.bfloat16)

def reference(pair_input, alignment_features, alignment_mask, token_valid, left_weight, right_weight, output_weight, gate_weight, up_weight, down_weight, kernel_weight):
    real_mask = alignment_mask.astype(jnp.float32)
    alignment_real = alignment_features.astype(jnp.float32)
    left_projected = (jnp.einsum('vdi,ie->vde', alignment_real, left_weight.astype(jnp.float32)) * real_mask[:, :, None]).astype(jnp.bfloat16)
    right_projected = (jnp.einsum('vdi,ie->vde', alignment_real, right_weight.astype(jnp.float32)) * real_mask[:, :, None]).astype(jnp.bfloat16)
    counts = jnp.dot(real_mask.T, real_mask, precision=lax.Precision.HIGHEST, preferred_element_type=jnp.float32)
    right_flat = right_projected.reshape(ALIGN_ROWS, TOKEN_COUNT * COPM)

    def outer_rows(first_row):
        left_part = lax.dynamic_slice_in_dim(left_projected, first_row, strip_rows, 1).reshape(ALIGN_ROWS, strip_rows * COPM)
        products = jnp.dot(left_part.T, right_flat, preferred_element_type=jnp.float32)
        products = products.reshape(strip_rows, COPM, TOKEN_COUNT, COPM).transpose(0, 2, 1, 3)
        products = products.reshape(strip_rows * TOKEN_COUNT, COPM * COPM).astype(jnp.bfloat16)
        update = jnp.dot(products, output_weight, preferred_element_type=jnp.float32).reshape(strip_rows, TOKEN_COUNT, CPAIR)
        pair_count = lax.dynamic_slice_in_dim(counts, first_row, strip_rows, 0)
        update = update / jnp.maximum(pair_count, 1.0)[:, :, None]
        base_pair = lax.dynamic_slice_in_dim(pair_input, first_row, strip_rows, 0).astype(jnp.float32)
        return (base_pair + update).astype(jnp.bfloat16)
    starts = jnp.arange(TOKEN_COUNT // strip_rows, dtype=jnp.int32) * strip_rows
    pair_one = lax.map(outer_rows, starts).reshape(TOKEN_COUNT, TOKEN_COUNT, CPAIR)

    def one_slab(pair_slab):
        return transition(pair_slab, gate_weight, up_weight, down_weight)
    pair_slabs = pair_one.reshape(TOKEN_COUNT * TOKEN_COUNT // slab_rows, slab_rows, CPAIR)
    pair_two = lax.map(one_slab, pair_slabs).reshape(TOKEN_COUNT, TOKEN_COUNT, CPAIR)
    pair_mirror = jnp.swapaxes(pair_two, 0, 1)
    pad_real = token_valid.astype(jnp.float32)
    symmetric = (pair_two.astype(jnp.float32) + pair_mirror.astype(jnp.float32)) * 0.5
    masked = (symmetric * pad_real[:, None, None] * pad_real[None, :, None]).astype(jnp.bfloat16)
    padded = jnp.pad(masked, ((1, 1), (1, 1), (0, 0)))

    def conv_rows(first_row):
        window = lax.dynamic_slice_in_dim(padded, first_row, strip_rows + 2, 0)
        summed = jnp.zeros((strip_rows * TOKEN_COUNT, CPAIR), jnp.float32)
        for shift_row in range(3):
            for shift_col in range(3):
                shifted = window[shift_row:shift_row + strip_rows, shift_col:shift_col + TOKEN_COUNT].reshape(strip_rows * TOKEN_COUNT, CPAIR)
                summed = summed + jnp.dot(shifted, kernel_weight[shift_row, shift_col], preferred_element_type=jnp.float32)
        centre = lax.dynamic_slice_in_dim(symmetric, first_row, strip_rows, 0).reshape(strip_rows * TOKEN_COUNT, CPAIR)
        return (centre + summed).astype(jnp.bfloat16).reshape(strip_rows, TOKEN_COUNT, CPAIR)
    return lax.map(conv_rows, starts).reshape(TOKEN_COUNT, TOKEN_COUNT, CPAIR)
```

```python
import functools
import math

import jax
import jax.numpy as jnp
from jax import lax
from jax.experimental import pallas as pl
from jax.experimental.pallas import tpu as pltpu
from jax.sharding import PartitionSpec as P

epsilon = 1e-05
lanes = 128
turns = 4
plane = ("col", "chan")
whole = ("row", "col", "chan")


def kernel_params(mib):
    return pltpu.CompilerParams(vmem_limit_bytes=mib * 1024 * 1024)


def outer_kernel(
    places, *refs, row_blocks, col_blocks, width, tokens_i, tokens_j, lane_at, row_at, mask_at, add
):
    row_refs, refs = refs[:row_blocks], refs[row_blocks:]
    col_refs, refs = refs[:col_blocks], refs[col_blocks:]
    weight, refs = refs[0], refs[1:]
    if add:
        base, refs = refs[0], refs[1:]
    out, lane_side, gathered, turned, row_side, scale, products, stacked = refs
    step = pl.program_id(0)
    strip = out.shape[0]
    groups = strip // turns
    high = width // turns
    depth = lane_side.shape[1]
    chunk = strip * width

    @pl.when(step == 0)
    def _():
        for n, block in enumerate(col_refs):
            count = block.shape[0]
            at = pl.ds(pl.multiple_of(places[row_blocks + n], 16), count)
            gathered[at, :] = block[:, row_at : row_at + tokens_j * width]
        for n in range(tokens_j * width // lanes):
            piece = gathered[:, n * lanes : (n + 1) * lanes].astype(jnp.float32)
            turned[n * lanes : (n + 1) * lanes, :] = piece.T
        for channel in range(width):
            spot = ((channel % turns) * high + channel // turns) * tokens_j
            rows = turned[pl.ds(channel, tokens_j, stride=width), :]
            row_side[spot : spot + tokens_j, :] = rows.astype(jnp.bfloat16)
        for n, block in enumerate(col_refs):
            count = block.shape[0]
            at = pl.ds(pl.multiple_of(places[row_blocks + n], 16), count)
            gathered[at, :lanes] = block[:, mask_at : mask_at + lanes]
        col_mask = gathered[:, :lanes]
        for n, block in enumerate(row_refs):
            count = block.shape[0]
            at = pl.ds(pl.multiple_of(places[n], 16), count)
            gathered[at, :lanes] = block[:, mask_at : mask_at + lanes]
        counts = lax.dot_general(
            col_mask,
            gathered[:, :lanes],
            (((0,), (0,)), ((), ())),
            preferred_element_type=jnp.float32,
        )[:tokens_j]
        inverse = 1.0 / jnp.maximum(counts, 1.0)
        for n in range(tokens_i // strip):
            scale[n, :, :strip] = inverse[:, n * strip : (n + 1) * strip]
        for n, block in enumerate(row_refs):
            count = block.shape[0]
            at = pl.ds(pl.multiple_of(places[n], 16), count)
            for g in range(tokens_i * width // lanes):
                piece = block[:, lane_at + g * lanes : lane_at + (g + 1) * lanes]
                lane_side[0, at, g * lanes : (g + 1) * lanes] = piece
                piece = piece.astype(jnp.float32)
                for turn in range(1, turns):
                    lane_side[turn, at, g * lanes : (g + 1) * lanes] = pltpu.roll(
                        piece, turn * width, 1
                    ).astype(jnp.bfloat16)

    span = high * tokens_j
    for turn in range(turns):
        products[turn] = jnp.dot(
            row_side[turn * span : (turn + 1) * span, :],
            lane_side[turn, :, pl.ds(pl.multiple_of(step * chunk, lanes), chunk)],
            preferred_element_type=jnp.float32,
        ).astype(jnp.bfloat16)
    position = lax.broadcasted_iota(jnp.int32, (tokens_j, lanes), 1) // width
    strip_scale = scale[step]
    for u in range(turns):
        for g in range(groups):
            for h in range(high):
                parts = [
                    products[
                        (t - u) % turns,
                        h * tokens_j : (h + 1) * tokens_j,
                        g * lanes : (g + 1) * lanes,
                    ]
                    for t in range(turns)
                ]
                mixed = parts[-1]
                for t in range(turns - 1):
                    mixed = jnp.where(position == t, parts[t], mixed)
                stacked[g * tokens_j : (g + 1) * tokens_j, h * lanes : (h + 1) * lanes] = mixed
        update = jnp.dot(stacked[...], weight[u], preferred_element_type=jnp.float32)
        for g in range(groups):
            i = turns * g + u
            value = update[g * tokens_j : (g + 1) * tokens_j] * strip_scale[:, i : i + 1]
            if add:
                value = value + base[i].astype(jnp.float32)
            out[i] = value.astype(out.dtype)


def outer_update(places, row_side, col_side, weight, base, sizes, swapped):
    tokens_i, tokens_j, width, channels = sizes
    strip = math.gcd(16, tokens_i)
    depth = sum(block.shape[0] for block in row_side)
    lane_at = tokens_i * width if swapped else 0
    row_at = 0 if swapped else tokens_j * width
    body = functools.partial(
        outer_kernel,
        row_blocks=len(row_side),
        col_blocks=len(col_side),
        width=width,
        tokens_i=tokens_i,
        tokens_j=tokens_j,
        lane_at=lane_at,
        row_at=row_at,
        mask_at=2 * tokens_i * width,
        add=base is not None,
    )
    if tokens_i != tokens_j:
        body = functools.partial(body, mask_at=0, lane_at=lane_at + lanes, row_at=row_at + lanes)
    whole_array = lambda a: pl.BlockSpec(a.shape, lambda n, rank=a.ndim: (0,) * rank)
    tile = pl.BlockSpec((strip, tokens_j, channels), lambda n: (n, 0, 0))
    operands = [*row_side, *col_side, weight]
    specs = [whole_array(a) for a in operands]
    if base is not None:
        operands.append(base)
        specs.append(tile)
    flops = 2 * tokens_i * tokens_j * width * width * (depth + channels)
    return pl.pallas_call(
        body,
        grid=(tokens_i // strip,),
        in_specs=[pl.BlockSpec(memory_space=pltpu.SMEM), *specs],
        out_specs=tile,
        out_shape=jax.ShapeDtypeStruct((tokens_i, tokens_j, channels), jnp.bfloat16),
        scratch_shapes=[
            pltpu.VMEM((turns, depth, tokens_i * width), jnp.bfloat16),
            pltpu.VMEM((depth, tokens_j * width), jnp.bfloat16),
            pltpu.VMEM((tokens_j * width, depth), jnp.float32),
            pltpu.VMEM((tokens_j * width, depth), jnp.bfloat16),
            pltpu.VMEM((tokens_i // strip, tokens_j, lanes), jnp.float32),
            pltpu.VMEM((turns, tokens_j * width // turns, strip * width), jnp.bfloat16),
            pltpu.VMEM((strip // turns * tokens_j, width * width), jnp.bfloat16),
        ],
        compiler_params=kernel_params(40),
        cost_estimate=pl.CostEstimate(flops=flops, bytes_accessed=4 << 20, transcendentals=0),
    )(places, *operands)


def transition_rows(values, gate_up, down):
    centre = jnp.mean(values, axis=-1, keepdims=True)
    offset = values - centre
    spread = jnp.mean(offset * offset, axis=-1, keepdims=True)
    normed = (offset * lax.rsqrt(spread + epsilon)).astype(jnp.bfloat16)
    both = jnp.dot(normed, gate_up, preferred_element_type=jnp.float32)
    hidden_width = gate_up.shape[1] // 2
    half, up = both[:, :hidden_width], both[:, hidden_width:]
    hidden = ((half + half * jnp.tanh(half)) * up).astype(jnp.bfloat16)
    return values + jnp.dot(hidden, down, preferred_element_type=jnp.float32)


def own_kernel(pair_one, gate_up, down, out):
    rows, columns, channels = out.shape
    values = pair_one[...].astype(jnp.float32).reshape(rows * columns, channels)
    result = transition_rows(values, gate_up[...], down[...])
    out[...] = result.astype(out.dtype).reshape(out.shape)


def mirror_kernel(base, update, pair_two, gate_up, down, out):
    rows, columns, channels = out.shape
    values = base[...].astype(jnp.float32) + update[...].astype(jnp.float32)
    values = values.astype(jnp.bfloat16).astype(jnp.float32).reshape(rows * columns, channels)
    result = transition_rows(values, gate_up[...], down[...]).astype(jnp.bfloat16)
    mirrored = result.astype(jnp.float32).reshape(out.shape)
    out[...] = ((pair_two[...].astype(jnp.float32) + mirrored) * 0.5).astype(out.dtype)


def run_transition(body, tiles, gate_up, down):
    rows, columns, channels = tiles[0].shape
    strip = max(1, math.gcd(rows, 512 // columns))
    tile = pl.BlockSpec((strip, columns, channels), lambda n: (n, 0, 0))
    fixed = lambda a: pl.BlockSpec(a.shape, lambda n: (0, 0))
    flops = 6 * rows * columns * channels * down.shape[0]
    return pl.pallas_call(
        body,
        grid=(rows // strip,),
        in_specs=[tile] * len(tiles) + [fixed(gate_up), fixed(down)],
        out_specs=tile,
        out_shape=jax.ShapeDtypeStruct((rows, columns, channels), jnp.bfloat16),
        compiler_params=kernel_params(40),
        cost_estimate=pl.CostEstimate(
            flops=flops, bytes_accessed=4 << 20, transcendentals=rows * columns * down.shape[0]
        ),
    )(*tiles, gate_up, down)


def conv_kernel(valid_i, symmetric, valid_j, top, bottom, left, right, weight, out, padded):
    step = pl.program_id(0)
    rows, columns, channels = symmetric.shape
    strip = out.shape[0]

    @pl.when(step == 0)
    def _():
        padded[0, 8 : 8 + columns, :] = top[...].astype(jnp.float32)
        padded[rows + 1, 8 : 8 + columns, :] = bottom[...].astype(jnp.float32)
        for i in range(rows):
            keep = valid_j[...] * valid_i[i].astype(jnp.float32)
            padded[i + 1, 8 : 8 + columns, :] = symmetric[i].astype(jnp.float32) * keep
        for i in range(rows + 2):
            padded[i, 7:8, :] = left[i : i + 1, :].astype(jnp.float32)
            padded[i, 8 + columns : 9 + columns, :] = right[i : i + 1, :].astype(jnp.float32)

    window = padded.at[pl.ds(step * strip, strip + 2)]
    shifted = [
        window[:, 7 + b : 7 + b + columns, :]
        .astype(jnp.bfloat16)
        .reshape((strip + 2) * columns, channels)
        for b in range(3)
    ]
    taps = jnp.dot(
        jnp.concatenate(shifted, axis=1), weight[...], preferred_element_type=jnp.float32
    ).reshape(strip + 2, columns, 3 * channels)
    total = symmetric[pl.ds(step * strip, strip)].astype(jnp.float32)
    for a in range(3):
        total = total + taps[a : a + strip, :, a * channels : (a + 1) * channels]
    out[...] = total.astype(out.dtype)


def convolve(symmetric, valid_i, valid_j, halos, kernel_weight):
    rows, columns, channels = symmetric.shape
    strip = math.gcd(16, rows)
    weight = kernel_weight.transpose(1, 2, 0, 3).reshape(3 * channels, 3 * channels)
    operands = [symmetric, valid_j, *halos, weight]
    fixed = lambda a: pl.BlockSpec(a.shape, lambda n, rank=a.ndim: (0,) * rank)
    return pl.pallas_call(
        conv_kernel,
        grid=(rows // strip,),
        in_specs=[pl.BlockSpec(memory_space=pltpu.SMEM)] + [fixed(a) for a in operands],
        out_specs=pl.BlockSpec((strip, columns, channels), lambda n: (n, 0, 0)),
        out_shape=jax.ShapeDtypeStruct(symmetric.shape, jnp.bfloat16),
        scratch_shapes=[pltpu.VMEM((rows + 2, columns + 16, channels), jnp.float32)],
        compiler_params=kernel_params(40),
        cost_estimate=pl.CostEstimate(
            flops=18 * rows * columns * channels * channels,
            bytes_accessed=3 << 20,
            transcendentals=0,
        ),
    )(valid_i, *operands)


def shifts(axis, size, step):
    return [(n, (n + step) % size) for n in range(size)]


def on_device(
    pair_input,
    alignment_features,
    alignment_mask,
    token_valid,
    left_weight,
    right_weight,
    output_weight,
    gate_weight,
    up_weight,
    down_weight,
    kernel_weight,
):
    rows_dev, cols_dev, channels = pair_input.shape
    local_rows, local_tokens, align_width = alignment_features.shape
    width = left_weight.shape[1]
    row_count, col_count = lax.axis_size("row"), lax.axis_size(plane)
    x_count, core_count = lax.axis_size("col"), lax.axis_size("chan")
    row_index, col_index = lax.axis_index("row"), lax.axis_index(plane)
    x_index, core_index = lax.axis_index("col"), lax.axis_index("chan")
    square = row_count == col_count
    mirror_pairs = [
        (r * col_count + c, c * col_count + r) for r in range(row_count) for c in range(col_count)
    ]

    flat = alignment_features.reshape(local_rows * local_tokens, align_width)
    mask_rows = alignment_mask.astype(jnp.float32)
    projected = []
    for weight in (left_weight, right_weight):
        value = jnp.dot(flat, weight, preferred_element_type=jnp.float32)
        value = value.reshape(local_rows, local_tokens, width) * mask_rows[:, :, None]
        projected.append(value.astype(jnp.bfloat16))
    mask_block = jnp.pad(
        alignment_mask.astype(jnp.bfloat16), ((0, 0), (0, lanes - local_tokens % lanes))
    )

    if square:
        block = jnp.concatenate(
            [p.reshape(local_rows, local_tokens * width) for p in projected] + [mask_block], axis=1
        )
        col_side, col_places = [block], [row_index]
        for step in range(1, row_count):
            col_side.append(lax.ppermute(block, "row", shifts("row", row_count, -step)))
            col_places.append((row_index + step) % row_count)
        first = lax.ppermute(block, whole, mirror_pairs)
        row_side, row_places = [first], [col_index]
        for step in range(1, x_count):
            row_side.append(lax.ppermute(first, "col", shifts("col", x_count, -step)))
            row_places.append(((x_index + step) % x_count) * core_count + core_index)
        for step in range(1, core_count):
            for n in range(x_count):
                row_side.append(
                    lax.ppermute(row_side[n], "chan", shifts("chan", core_count, -step))
                )
                row_places.append(
                    ((x_index + n) % x_count) * core_count + (core_index + step) % core_count
                )
        places = jnp.stack(row_places + col_places).astype(jnp.int32) * local_rows
        mirrored_input = lax.ppermute(jnp.swapaxes(pair_input, 0, 1), whole, mirror_pairs)
    else:
        block = jnp.stack(projected, axis=2)
        col_full = lax.all_gather(block, "row", axis=0, tiled=True)
        col_mask = lax.all_gather(mask_block, "row", axis=0, tiled=True)
        wide = lax.all_gather(block, plane, axis=1, tiled=True)
        row_full = lax.all_to_all(wide, "row", split_axis=1, concat_axis=0, tiled=True)
        wide_mask = lax.all_gather(mask_block[:, :local_tokens], plane, axis=1, tiled=True)
        row_mask = lax.all_to_all(wide_mask, "row", split_axis=1, concat_axis=0, tiled=True)
        row_mask = jnp.pad(row_mask, ((0, 0), (0, lanes - rows_dev % lanes)))
        depth = row_full.shape[0]

        def laid_out(mask, full):
            sides = [full[:, :, n].reshape(depth, full.shape[1] * width) for n in range(2)]
            return [jnp.concatenate([mask] + sides, axis=1)]

        row_side, col_side = laid_out(row_mask, row_full), laid_out(col_mask, col_full)
        places = jnp.zeros((2,), jnp.int32)
        share = rows_dev // col_count
        fold = row_count // col_count
        second = lax.all_to_all(
            lax.all_to_all(pair_input, plane, split_axis=0, concat_axis=1, tiled=True),
            "row",
            split_axis=1,
            concat_axis=0,
            tiled=True,
        )
        third = lax.all_to_all(
            jnp.swapaxes(second, 0, 1), plane, split_axis=1, concat_axis=1, tiled=True
        )
        mirrored_input = (
            third.reshape(rows_dev, col_count, fold, share, channels)
            .transpose(0, 2, 1, 3, 4)
            .reshape(rows_dev, cols_dev, channels)
        )

    def ordered(weight):
        split = weight.reshape(width // turns, turns, width, channels)
        return jnp.stack(
            [jnp.roll(split, u, axis=1).reshape(width * width, channels) for u in range(turns)]
        )

    by_pair = output_weight.reshape(width, width, channels)
    own_weight = ordered(jnp.swapaxes(by_pair, 0, 1))
    mirror_weight = ordered(by_pair)
    gate_up = jnp.concatenate([gate_weight * 0.5, up_weight], axis=1).astype(jnp.bfloat16)

    sizes = (rows_dev, cols_dev, width, channels)
    pair_one = outer_update(places, row_side, col_side, own_weight, pair_input, sizes, False)
    mirror_update = outer_update(places, row_side, col_side, mirror_weight, None, sizes, True)
    pair_two = run_transition(own_kernel, [pair_one], gate_up, down_weight)
    symmetric = run_transition(
        mirror_kernel, [mirrored_input, mirror_update, pair_two], gate_up, down_weight
    )

    valid_i = lax.dynamic_slice_in_dim(token_valid, row_index * rows_dev, rows_dev)
    valid_j = lax.dynamic_slice_in_dim(token_valid, col_index * cols_dev, cols_dev)
    keep_i = valid_i.astype(jnp.bfloat16)[:, None]
    keep_j = valid_j.astype(jnp.bfloat16)[:, None]
    edge = lambda j: symmetric[:, j] * keep_i * keep_j[j]
    ahead = lambda size: [(n, n + 1) for n in range(size - 1)]
    back = lambda size: [(n + 1, n) for n in range(size - 1)]
    left = lax.ppermute(edge(cols_dev - 1), plane, ahead(col_count))
    right = lax.ppermute(edge(0), plane, back(col_count))

    def border(i):
        line = symmetric[i] * keep_j * keep_i[i]
        return jnp.concatenate([left[i : i + 1], line, right[i : i + 1]], axis=0)

    top = lax.ppermute(border(rows_dev - 1), "row", ahead(row_count))
    bottom = lax.ppermute(border(0), "row", back(row_count))
    left = jnp.concatenate([top[:1], left, bottom[:1]], axis=0)
    right = jnp.concatenate([top[-1:], right, bottom[-1:]], axis=0)
    wide_valid = jnp.broadcast_to(valid_j.astype(jnp.float32)[:, None], (cols_dev, channels))
    return convolve(
        symmetric, valid_i, wide_valid, [top[1:-1], bottom[1:-1], left, right], kernel_weight
    )


def solution(mesh):
    placed = (
        P(("groups", "row"), plane, None),
        P("row", ("groups", "col", "chan"), None),
        P("row", ("groups", "col", "chan")),
        P("groups"),
        P(),
        P(),
        P(),
        P(),
        P(),
        P(),
        P(),
    )
    return jax.shard_map(
        on_device,
        mesh=mesh,
        in_specs=placed,
        out_specs=P(("groups", "row"), plane, None),
        check_vma=False,
    )
```

```python
import functools
import math

import jax
import jax.numpy as jnp
from jax import lax
from jax.experimental import pallas as pl
from jax.experimental.pallas import tpu as pltpu
from jax.sharding import PartitionSpec as P

epsilon = 1e-05
lanes = 128
turns = 4
plane = ("col", "chan")
whole = ("row", "col", "chan")
unit = 16


def kernel_params(mib):
    return pltpu.CompilerParams(vmem_limit_bytes=mib * 1024 * 1024)


def arrange_kernel(
    places, *refs, row_blocks, col_blocks, width, tokens_row, tokens_col
):
    row_refs, refs = refs[:row_blocks], refs[row_blocks:]
    col_refs, refs = refs[:col_blocks], refs[col_blocks:]
    row_side, lane_side, scale, gathered, turned, row_mask, col_mask = refs
    high = width // turns
    row_span, col_span = tokens_row * width, tokens_col * width
    for n, block in enumerate(row_refs):
        at = pl.ds(pl.multiple_of(places[n], 16), block.shape[0])
        gathered[at, :] = block[:, :row_span]
        row_mask[at, :] = block[:, row_span:]
    for n, block in enumerate(col_refs):
        at = pl.ds(pl.multiple_of(places[row_blocks + n], 16), block.shape[0])
        col_mask[at, :] = block[:, col_span:]
        for g in range(col_span // lanes):
            spot = slice(g * lanes, (g + 1) * lanes)
            piece = block[:, spot]
            lane_side[0, at, spot] = piece
            piece = piece.astype(jnp.float32)
            for turn in range(1, turns):
                lane_side[turn, at, spot] = pltpu.roll(piece, turn * width, 1).astype(jnp.bfloat16)
    for n in range(row_span // lanes):
        spot = slice(n * lanes, (n + 1) * lanes)
        turned[spot, :] = gathered[:, spot].astype(jnp.float32).T
    for channel in range(width):
        spot = ((channel % turns) * high + channel // turns) * tokens_row
        rows = turned[pl.ds(channel, tokens_row, stride=width), :]
        row_side[spot : spot + tokens_row, :] = rows.astype(jnp.bfloat16)
    counts = lax.dot_general(
        row_mask[...],
        col_mask[...],
        (((0,), (0,)), ((), ())),
        preferred_element_type=jnp.float32,
    )[:tokens_row]
    inverse = 1.0 / jnp.maximum(counts, 1.0)
    strip = scale.shape[0]
    for n in range(strip):
        count = tokens_col // strip
        scale[n, :, :count] = inverse[:, n * count : (n + 1) * count]


def arrange(places, row_side, col_side, width, tokens_row, tokens_col):
    depth = sum(block.shape[0] for block in row_side)
    body = functools.partial(
        arrange_kernel,
        row_blocks=len(row_side),
        col_blocks=len(col_side),
        width=width,
        tokens_row=tokens_row,
        tokens_col=tokens_col,
    )
    in_vmem = pl.BlockSpec(memory_space=pltpu.VMEM)
    return pl.pallas_call(
        body,
        in_specs=[pl.BlockSpec(memory_space=pltpu.SMEM)]
        + [in_vmem] * (len(row_side) + len(col_side)),
        out_specs=[in_vmem] * 3,
        out_shape=[
            jax.ShapeDtypeStruct((tokens_row * width, depth), jnp.bfloat16),
            jax.ShapeDtypeStruct((turns, depth, tokens_col * width), jnp.bfloat16),
            jax.ShapeDtypeStruct((tokens_col // unit, tokens_row, lanes), jnp.float32),
        ],
        scratch_shapes=[
            pltpu.VMEM((depth, tokens_row * width), jnp.bfloat16),
            pltpu.VMEM((tokens_row * width, depth), jnp.float32),
            pltpu.VMEM((depth, lanes), jnp.bfloat16),
            pltpu.VMEM((depth, lanes), jnp.bfloat16),
        ],
        compiler_params=kernel_params(12),
        cost_estimate=pl.CostEstimate(flops=1 << 24, bytes_accessed=4 << 20, transcendentals=0),
    )(places, *row_side, *col_side)


def transition_rows(values, gate_up, down):
    channels = values.shape[1]
    mean_of = jnp.full((channels, channels), 1.0 / channels, jnp.bfloat16)
    centre = jnp.dot(values.astype(jnp.bfloat16), mean_of, preferred_element_type=jnp.float32)
    offset = values - centre
    squares = (offset * offset).astype(jnp.bfloat16)
    spread = jnp.dot(squares, mean_of, preferred_element_type=jnp.float32)
    normed = (offset * lax.rsqrt(spread + epsilon)).astype(jnp.bfloat16)
    both = jnp.dot(normed, gate_up, preferred_element_type=jnp.float32)
    hidden_width = gate_up.shape[1] // 2
    half, up = both[:, :hidden_width], both[:, hidden_width:]
    hidden = ((half + half * jnp.tanh(half)) * up).astype(jnp.bfloat16)
    return values + jnp.dot(hidden, down, preferred_element_type=jnp.float32)


def tile_kernel(
    row_side, lane_side, scale, base, weight, gate_up, down, out, products, stacked, held
):
    strip, tokens_row, channels = out.shape
    width = lane_side.shape[2] // strip
    high = width // turns
    groups = strip // turns
    span = high * tokens_row
    for turn in range(turns):
        products[turn] = jnp.dot(
            row_side[turn * span : (turn + 1) * span, :],
            lane_side[turn],
            preferred_element_type=jnp.float32,
        ).astype(jnp.bfloat16)
    position = lax.broadcasted_iota(jnp.int32, (tokens_row, lanes), 1) // width
    for g in range(groups):
        for h in range(high):
            parts = [
                products[t, h * tokens_row : (h + 1) * tokens_row, g * lanes : (g + 1) * lanes]
                for t in range(turns)
            ]
            for u in range(turns):
                mixed = parts[(turns - 1 - u) % turns]
                for t in range(turns - 1):
                    mixed = jnp.where(position == t, parts[(t - u) % turns], mixed)
                stacked[
                    u, g * tokens_row : (g + 1) * tokens_row, h * lanes : (h + 1) * lanes
                ] = mixed
    for u in range(turns):
        update = jnp.dot(stacked[u], weight[u], preferred_element_type=jnp.float32)
        for g in range(groups):
            n = turns * g + u
            factor = scale[n // unit][:, n % unit : n % unit + 1]
            value = update[g * tokens_row : (g + 1) * tokens_row] * factor
            value = base[n].astype(jnp.float32) + value
            held[n * tokens_row : (n + 1) * tokens_row, :] = value.astype(jnp.bfloat16)
    piece = min(16, strip)
    for first in range(0, strip, piece):
        at = slice(first * tokens_row, (first + piece) * tokens_row)
        result = transition_rows(held[at, :].astype(jnp.float32), gate_up[...], down[...])
        out[first : first + piece] = result.astype(out.dtype).reshape(piece, tokens_row, channels)


def tile_strips(first, count, strip, row_side, lane_side, scale, base, weight, gate_up, down):
    tokens_row, channels = base.shape[1:]
    turn_count, depth, span = lane_side.shape
    width = span // base.shape[0]
    start = first // strip
    fixed = lambda a: pl.BlockSpec(a.shape, lambda n, rank=a.ndim: (0,) * rank)
    flops = 2 * count * tokens_row * (width * width * (depth + channels) + 3 * channels * 512)
    return pl.pallas_call(
        tile_kernel,
        grid=(count // strip,),
        in_specs=[
            fixed(row_side),
            pl.BlockSpec((turn_count, depth, strip * width), lambda n: (0, 0, n + start)),
            pl.BlockSpec((strip // unit, tokens_row, lanes), lambda n: (n + start, 0, 0)),
            pl.BlockSpec((strip, tokens_row, channels), lambda n: (n + start, 0, 0)),
            fixed(weight),
            fixed(gate_up),
            fixed(down),
        ],
        out_specs=pl.BlockSpec((strip, tokens_row, channels), lambda n: (n, 0, 0)),
        out_shape=jax.ShapeDtypeStruct((count, tokens_row, channels), jnp.bfloat16),
        scratch_shapes=[
            pltpu.VMEM((turns, tokens_row * width // turns, strip * width), jnp.bfloat16),
            pltpu.VMEM((turns, strip // turns * tokens_row, width * width), jnp.bfloat16),
            pltpu.VMEM((strip * tokens_row, channels), jnp.bfloat16),
        ],
        compiler_params=kernel_params(40),
        cost_estimate=pl.CostEstimate(flops=flops, bytes_accessed=4 << 20, transcendentals=0),
    )(row_side, lane_side, scale, base, weight, gate_up, down)


def conv_kernel(
    valid_i, pair_two, *refs, parts
):
    counts = [len(p) for p in parts]
    total_parts = sum(counts)
    mirrored, refs = refs[:total_parts], refs[total_parts:]
    valid_j, top, bottom, left, right, weight, out, padded, centre = refs
    step = pl.program_id(0)
    rows, columns, channels = pair_two.shape
    strip = out.shape[0]

    @pl.when(step == 0)
    def _():
        padded[0, 8 : 8 + columns, :] = top[...].astype(jnp.float32)
        padded[rows + 1, 8 : 8 + columns, :] = bottom[...].astype(jnp.float32)
        i = 0
        used = 0
        for count in counts:
            group = mirrored[used : used + count]
            used += count
            for n in range(group[0].shape[0]):
                other = group[0][n].astype(jnp.float32)
                for more in group[1:]:
                    other = other + more[n].astype(jnp.float32)
                symmetric = (pair_two[i].astype(jnp.float32) + other) * 0.5
                centre[i] = symmetric
                keep = valid_j[...] * valid_i[i].astype(jnp.float32)
                padded[i + 1, 8 : 8 + columns, :] = symmetric * keep
                i += 1
        for i in range(rows + 2):
            padded[i, 7:8, :] = left[i : i + 1, :].astype(jnp.float32)
            padded[i, 8 + columns : 9 + columns, :] = right[i : i + 1, :].astype(jnp.float32)

    window = padded.at[pl.ds(step * strip, strip + 2)]
    shifted = [
        window[:, 7 + b : 7 + b + columns, :]
        .astype(jnp.bfloat16)
        .reshape((strip + 2) * columns, channels)
        for b in range(3)
    ]
    taps = jnp.dot(
        jnp.concatenate(shifted, axis=1), weight[...], preferred_element_type=jnp.float32
    ).reshape(strip + 2, columns, 3 * channels)
    total = centre[pl.ds(step * strip, strip)]
    for a in range(3):
        total = total + taps[a : a + strip, :, a * channels : (a + 1) * channels]
    out[...] = total.astype(out.dtype)


def convolve(pair_two, mirrored, valid_i, valid_j, halos, weight):
    rows, columns, channels = pair_two.shape
    strip = math.gcd(32, rows)
    operands = [pair_two, *[a for part in mirrored for a in part], valid_j, *halos, weight]
    fixed = lambda a: pl.BlockSpec(a.shape, lambda n, rank=a.ndim: (0,) * rank)
    return pl.pallas_call(
        functools.partial(conv_kernel, parts=[tuple(range(len(part))) for part in mirrored]),
        grid=(rows // strip,),
        in_specs=[pl.BlockSpec(memory_space=pltpu.SMEM)] + [fixed(a) for a in operands],
        out_specs=pl.BlockSpec((strip, columns, channels), lambda n: (n, 0, 0)),
        out_shape=jax.ShapeDtypeStruct(pair_two.shape, jnp.bfloat16),
        scratch_shapes=[
            pltpu.VMEM((rows + 2, columns + 16, channels), jnp.float32),
            pltpu.VMEM((rows, columns, channels), jnp.float32),
        ],
        compiler_params=kernel_params(40),
        cost_estimate=pl.CostEstimate(
            flops=18 * rows * columns * channels * channels,
            bytes_accessed=3 << 20,
            transcendentals=0,
        ),
    )(valid_i, *operands)


def shifts(size, step):
    return [(n, (n + step) % size) for n in range(size)]


def on_device(
    pair_input,
    alignment_features,
    alignment_mask,
    token_valid,
    left_weight,
    right_weight,
    output_weight,
    gate_weight,
    up_weight,
    down_weight,
    kernel_weight,
):
    rows_dev, cols_dev, channels = pair_input.shape
    local_rows, local_tokens, align_width = alignment_features.shape
    width = left_weight.shape[1]
    row_count, col_count = lax.axis_size("row"), lax.axis_size(plane)
    x_count, core_count = lax.axis_size("col"), lax.axis_size("chan")
    row_index, col_index = lax.axis_index("row"), lax.axis_index(plane)
    x_index, core_index = lax.axis_index("col"), lax.axis_index("chan")
    square = row_count == col_count
    tiles = [(r, c) for r in range(row_count) for c in range(col_count)]
    place_of = lambda r, c: r * col_count + c

    flat = alignment_features.reshape(local_rows * local_tokens, align_width)
    mask_rows = alignment_mask.astype(jnp.float32)
    projected = []
    for weight in (left_weight, right_weight):
        value = jnp.dot(flat, weight, preferred_element_type=jnp.float32)
        value = value.reshape(local_rows, local_tokens, width) * mask_rows[:, :, None]
        projected.append(value.astype(jnp.bfloat16))
    narrow_mask = alignment_mask.astype(jnp.bfloat16)

    def beside(side, mask):
        depth, tokens = mask.shape
        room = jnp.pad(mask, ((0, 0), (0, lanes - tokens % lanes)))
        return jnp.concatenate([side.reshape(depth, tokens * width), room], axis=1)

    if square:
        left_block, right_block = (beside(side, narrow_mask) for side in projected)
        mirror_pairs = [(place_of(r, c), place_of(c, r)) for r, c in tiles]
        first = lax.ppermute(left_block, whole, mirror_pairs)
        col_side, col_places = [right_block], [row_index]
        for step in range(1, row_count):
            col_side.append(lax.ppermute(right_block, "row", shifts(row_count, -step)))
            col_places.append((row_index + step) % row_count)
        row_side, row_places = [first], [col_index]
        for step in range(1, x_count):
            row_side.append(lax.ppermute(first, "col", shifts(x_count, -step)))
            row_places.append(((x_index + step) % x_count) * core_count + core_index)
        for step in range(1, core_count):
            for n in range(x_count):
                row_side.append(lax.ppermute(row_side[n], "chan", shifts(core_count, -step)))
                row_places.append(
                    ((x_index + n) % x_count) * core_count + (core_index + step) % core_count
                )
        places = jnp.stack(row_places + col_places).astype(jnp.int32) * local_rows
    else:
        left_wide = lax.all_gather(projected[0], plane, axis=1, tiled=True)
        mask_wide = lax.all_gather(narrow_mask, plane, axis=1, tiled=True)
        turn = lambda a: lax.all_to_all(a, "row", split_axis=1, concat_axis=0, tiled=True)
        gather = lambda a: lax.all_gather(a, "row", axis=0, tiled=True)
        row_side = [beside(turn(left_wide), turn(mask_wide))]
        col_side = [beside(gather(projected[1]), gather(narrow_mask))]
        places = jnp.zeros((2,), jnp.int32)

    split = output_weight.reshape(width // turns, turns, width, channels)
    weight = jnp.stack(
        [jnp.roll(split, u, axis=1).reshape(width * width, channels) for u in range(turns)]
    )
    gate_up = jnp.concatenate([gate_weight * 0.5, up_weight], axis=1).astype(jnp.bfloat16)
    conv_weight = kernel_weight.transpose(1, 2, 0, 3).reshape(3 * channels, 3 * channels)
    base = jnp.swapaxes(pair_input, 0, 1)

    sides = arrange(places, row_side, col_side, width, rows_dev, cols_dev)
    run = lambda first, count, strip: tile_strips(
        first, count, strip, *sides, base, weight, gate_up, down_weight
    )
    ahead = lambda size: [(n, n + 1) for n in range(size - 1)]
    back = lambda size: [(n + 1, n) for n in range(size - 1)]

    if square and cols_dev % (4 * unit) == 0 and x_count > 1:
        part = cols_dev // 4
        host = lambda r, c: place_of(r, (r // core_count) * core_count + c % core_count)
        away = [(r, c) for r, c in tiles if r // core_count != c // core_count]
        near = [(r, c) for r, c in tiles if r // core_count == c // core_count]
        to_host = [(place_of(r, c), host(r, c)) for r, c in away]
        from_host = [(host(r, c), place_of(c, r)) for r, c in away]
        beside_pairs = [(place_of(r, c), place_of(c, r)) for r, c in near]
        send = lambda value, pairs: lax.ppermute(value, whole, pairs)
        sent, mirrored = [], []
        for n in range(2):
            strip = run(n * part, part, part)
            sent.append(strip)
            mirrored.append(
                [send(send(strip, to_host), from_host), send(strip, beside_pairs)]
            )
        strip = run(2 * part, 2 * part, 2 * part)
        sent.append(strip)
        turned = jnp.concatenate(sent, axis=0)
        edges = jnp.stack([turned[0], turned[-1], turned[:, 0], turned[:, -1]])
        edges = send(edges, mirror_pairs)
        mirrored.append([send(strip, mirror_pairs)])
    else:
        turned = run(0, cols_dev, math.gcd(unit, cols_dev))
        share = rows_dev // col_count
        fold = row_count // col_count
        second = lax.all_to_all(
            lax.all_to_all(
                jnp.swapaxes(turned, 0, 1), plane, split_axis=0, concat_axis=1, tiled=True
            ),
            "row",
            split_axis=1,
            concat_axis=0,
            tiled=True,
        )
        third = lax.all_to_all(
            jnp.swapaxes(second, 0, 1), plane, split_axis=1, concat_axis=1, tiled=True
        )
        full = (
            third.reshape(rows_dev, col_count, fold, share, channels)
            .transpose(0, 2, 1, 3, 4)
            .reshape(rows_dev, cols_dev, channels)
        )
        mirrored = [[full]]
        edges = (full[0], full[-1], full[:, 0], full[:, -1])

    pair_two = jnp.swapaxes(turned, 0, 1)
    valid_i = lax.dynamic_slice_in_dim(token_valid, row_index * rows_dev, rows_dev)
    valid_j = lax.dynamic_slice_in_dim(token_valid, col_index * cols_dev, cols_dev)
    keep_i = valid_i.astype(jnp.float32)[:, None]
    keep_j = valid_j.astype(jnp.float32)[:, None]
    mean = lambda a, b: (a.astype(jnp.float32) + b.astype(jnp.float32)) * 0.5
    last_i, last_j = rows_dev - 1, cols_dev - 1
    first_line = (mean(turned[:, 0], edges[0]) * keep_j * keep_i[0]).astype(jnp.bfloat16)
    last_line = (mean(turned[:, -1], edges[1]) * keep_j * keep_i[last_i]).astype(jnp.bfloat16)
    first_side = (mean(turned[0], edges[2]) * keep_i * keep_j[0]).astype(jnp.bfloat16)
    last_side = (mean(turned[-1], edges[3]) * keep_i * keep_j[last_j]).astype(jnp.bfloat16)
    left = lax.ppermute(last_side, plane, ahead(col_count))
    right = lax.ppermute(first_side, plane, back(col_count))
    border = lambda i, line: jnp.concatenate([left[i][None], line, right[i][None]], axis=0)
    top = lax.ppermute(border(last_i, last_line), "row", ahead(row_count))
    bottom = lax.ppermute(border(0, first_line), "row", back(row_count))
    left = jnp.concatenate([top[:1], left, bottom[:1]], axis=0)
    right = jnp.concatenate([top[-1:], right, bottom[-1:]], axis=0)
    wide_valid = jnp.broadcast_to(keep_j, (cols_dev, channels))
    return convolve(
        pair_two,
        mirrored,
        valid_i,
        wide_valid,
        [top[1:-1], bottom[1:-1], left, right],
        conv_weight,
    )


def solution(mesh):
    placed = (
        P(("groups", "row"), plane, None),
        P("row", ("groups", "col", "chan"), None),
        P("row", ("groups", "col", "chan")),
        P("groups"),
        P(),
        P(),
        P(),
        P(),
        P(),
        P(),
        P(),
    )
    return jax.shard_map(
        on_device,
        mesh=mesh,
        in_specs=placed,
        out_specs=P(("groups", "row"), plane, None),
        check_vma=False,
    )
```

```python
import functools
import math

import jax
import jax.numpy as jnp
from jax import lax
from jax.experimental import pallas as pl
from jax.experimental.pallas import tpu as pltpu
from jax.sharding import PartitionSpec as P

epsilon = 1e-05
lanes = 128
turns = 4
plane = ("col", "chan")
whole = ("row", "col", "chan")
unit = 8


def kernel_params(mib):
    return pltpu.CompilerParams(vmem_limit_bytes=mib * 1024 * 1024)


def arrange_kernel(
    places, *refs, row_blocks, col_blocks, width, tokens_row, tokens_col
):
    row_refs, refs = refs[:row_blocks], refs[row_blocks:]
    col_refs, refs = refs[:col_blocks], refs[col_blocks:]
    row_side, lane_side, scale, gathered, turned, row_mask, col_mask = refs
    high = width // turns
    row_span, col_span = tokens_row * width, tokens_col * width
    for n, block in enumerate(row_refs):
        at = pl.ds(pl.multiple_of(places[n], 16), block.shape[0])
        gathered[at, :] = block[:, :row_span]
        row_mask[at, :] = block[:, row_span:]
    for n, block in enumerate(col_refs):
        at = pl.ds(pl.multiple_of(places[row_blocks + n], 16), block.shape[0])
        col_mask[at, :] = block[:, col_span:]
        for g in range(col_span // lanes):
            spot = slice(g * lanes, (g + 1) * lanes)
            piece = block[:, spot]
            lane_side[0, at, spot] = piece
            piece = piece.astype(jnp.float32)
            for turn in range(1, turns):
                lane_side[turn, at, spot] = pltpu.roll(piece, turn * width, 1).astype(jnp.bfloat16)
    for n in range(row_span // lanes):
        spot = slice(n * lanes, (n + 1) * lanes)
        turned[spot, :] = gathered[:, spot].astype(jnp.float32).T
    for channel in range(width):
        spot = ((channel % turns) * high + channel // turns) * tokens_row
        rows = turned[pl.ds(channel, tokens_row, stride=width), :]
        row_side[spot : spot + tokens_row, :] = rows.astype(jnp.bfloat16)
    counts = lax.dot_general(
        row_mask[...],
        col_mask[...],
        (((0,), (0,)), ((), ())),
        preferred_element_type=jnp.float32,
    )[:tokens_row]
    inverse = 1.0 / jnp.maximum(counts, 1.0)
    strip = scale.shape[0]
    for n in range(strip):
        count = tokens_col // strip
        scale[n, :, :count] = inverse[:, n * count : (n + 1) * count]


def arrange(places, row_side, col_side, width, tokens_row, tokens_col):
    depth = sum(block.shape[0] for block in row_side)
    body = functools.partial(
        arrange_kernel,
        row_blocks=len(row_side),
        col_blocks=len(col_side),
        width=width,
        tokens_row=tokens_row,
        tokens_col=tokens_col,
    )
    in_vmem = pl.BlockSpec(memory_space=pltpu.VMEM)
    return pl.pallas_call(
        body,
        in_specs=[pl.BlockSpec(memory_space=pltpu.SMEM)]
        + [in_vmem] * (len(row_side) + len(col_side)),
        out_specs=[in_vmem] * 3,
        out_shape=[
            jax.ShapeDtypeStruct((tokens_row * width, depth), jnp.bfloat16),
            jax.ShapeDtypeStruct((turns, depth, tokens_col * width), jnp.bfloat16),
            jax.ShapeDtypeStruct((tokens_col // unit, tokens_row, lanes), jnp.float32),
        ],
        scratch_shapes=[
            pltpu.VMEM((depth, tokens_row * width), jnp.bfloat16),
            pltpu.VMEM((tokens_row * width, depth), jnp.float32),
            pltpu.VMEM((depth, lanes), jnp.bfloat16),
            pltpu.VMEM((depth, lanes), jnp.bfloat16),
        ],
        compiler_params=kernel_params(12),
        cost_estimate=pl.CostEstimate(flops=1024, bytes_accessed=1024, transcendentals=0),
    )(places, *row_side, *col_side)


def transition_rows(values, gate_up, down):
    channels = values.shape[1]
    mean_of = jnp.full((channels, channels), 1.0 / channels, jnp.bfloat16)
    centre = jnp.dot(values.astype(jnp.bfloat16), mean_of, preferred_element_type=jnp.float32)
    offset = values - centre
    squares = (offset * offset).astype(jnp.bfloat16)
    spread = jnp.dot(squares, mean_of, preferred_element_type=jnp.float32)
    normed = (offset * lax.rsqrt(spread + epsilon)).astype(jnp.bfloat16)
    both = jnp.dot(normed, gate_up, preferred_element_type=jnp.float32)
    hidden_width = gate_up.shape[1] // 2
    half, up = both[:, :hidden_width], both[:, hidden_width:]
    hidden = ((half + half * jnp.tanh(half)) * up).astype(jnp.bfloat16)
    return values + jnp.dot(hidden, down, preferred_element_type=jnp.float32)


def tile_kernel(
    row_side, lane_side, scale, base, weight, gate_up, down, out, products, stacked, held
):
    strip, tokens_row, channels = out.shape
    width = lane_side.shape[2] // strip
    high = width // turns
    groups = strip // turns
    span = high * tokens_row
    for turn in range(turns):
        products[turn] = jnp.dot(
            row_side[turn * span : (turn + 1) * span, :],
            lane_side[turn],
            preferred_element_type=jnp.float32,
        ).astype(jnp.bfloat16)
    position = lax.broadcasted_iota(jnp.int32, (tokens_row, lanes), 1) // width
    for g in range(groups):
        for h in range(high):
            parts = [
                products[t, h * tokens_row : (h + 1) * tokens_row, g * lanes : (g + 1) * lanes]
                for t in range(turns)
            ]
            for u in range(turns):
                mixed = parts[(turns - 1 - u) % turns]
                for t in range(turns - 1):
                    mixed = jnp.where(position == t, parts[(t - u) % turns], mixed)
                stacked[
                    u, g * tokens_row : (g + 1) * tokens_row, h * lanes : (h + 1) * lanes
                ] = mixed
    for u in range(turns):
        update = jnp.dot(stacked[u], weight[u], preferred_element_type=jnp.float32)
        for g in range(groups):
            n = turns * g + u
            factor = scale[n // unit][:, n % unit : n % unit + 1]
            value = update[g * tokens_row : (g + 1) * tokens_row] * factor
            value = base[n].astype(jnp.float32) + value
            held[n * tokens_row : (n + 1) * tokens_row, :] = value.astype(jnp.bfloat16)
    piece = math.gcd(strip, 24) if strip > 24 else strip
    for first in range(0, strip, piece):
        at = slice(first * tokens_row, (first + piece) * tokens_row)
        result = transition_rows(held[at, :].astype(jnp.float32), gate_up[...], down[...])
        out[first : first + piece] = result.astype(out.dtype).reshape(piece, tokens_row, channels)


def tile_strips(first, count, strip, row_side, lane_side, scale, base, weight, gate_up, down):
    tokens_row, channels = base.shape[1:]
    turn_count, depth, span = lane_side.shape
    width = span // base.shape[0]
    start = first // strip
    fixed = lambda a: pl.BlockSpec(a.shape, lambda n, rank=a.ndim: (0,) * rank)
    return pl.pallas_call(
        tile_kernel,
        grid=(count // strip,),
        in_specs=[
            fixed(row_side),
            pl.BlockSpec((turn_count, depth, strip * width), lambda n: (0, 0, n + start)),
            pl.BlockSpec((strip // unit, tokens_row, lanes), lambda n: (n + start, 0, 0)),
            pl.BlockSpec((strip, tokens_row, channels), lambda n: (n + start, 0, 0)),
            fixed(weight),
            fixed(gate_up),
            fixed(down),
        ],
        out_specs=pl.BlockSpec((strip, tokens_row, channels), lambda n: (n, 0, 0)),
        out_shape=jax.ShapeDtypeStruct((count, tokens_row, channels), jnp.bfloat16),
        scratch_shapes=[
            pltpu.VMEM((turns, tokens_row * width // turns, strip * width), jnp.bfloat16),
            pltpu.VMEM((turns, strip // turns * tokens_row, width * width), jnp.bfloat16),
            pltpu.VMEM((strip * tokens_row, channels), jnp.bfloat16),
        ],
        compiler_params=kernel_params(40),
        cost_estimate=pl.CostEstimate(flops=1024, bytes_accessed=1024, transcendentals=0),
    )(row_side, lane_side, scale, base, weight, gate_up, down)


def conv_kernel(
    valid_i, pair_two, *refs, parts
):
    counts = [len(p) for p in parts]
    total_parts = sum(counts)
    mirrored, refs = refs[:total_parts], refs[total_parts:]
    valid_j, top, bottom, left, right, weight, out, padded, centre = refs
    step = pl.program_id(0)
    rows, columns, channels = pair_two.shape
    strip = out.shape[0]

    @pl.when(step == 0)
    def _():
        padded[0, 8 : 8 + columns, :] = top[...].astype(jnp.float32)
        padded[rows + 1, 8 : 8 + columns, :] = bottom[...].astype(jnp.float32)
        i = 0
        used = 0
        for count in counts:
            group = mirrored[used : used + count]
            used += count
            for n in range(group[0].shape[0]):
                other = group[0][n].astype(jnp.float32)
                for more in group[1:]:
                    other = other + more[n].astype(jnp.float32)
                symmetric = (pair_two[i].astype(jnp.float32) + other) * 0.5
                centre[i] = symmetric
                keep = valid_j[...] * valid_i[i].astype(jnp.float32)
                padded[i + 1, 8 : 8 + columns, :] = symmetric * keep
                i += 1
        for i in range(rows + 2):
            padded[i, 7:8, :] = left[i : i + 1, :].astype(jnp.float32)
            padded[i, 8 + columns : 9 + columns, :] = right[i : i + 1, :].astype(jnp.float32)

    window = padded.at[pl.ds(step * strip, strip + 2)]
    shifted = [
        window[:, 7 + b : 7 + b + columns, :]
        .astype(jnp.bfloat16)
        .reshape((strip + 2) * columns, channels)
        for b in range(3)
    ]
    taps = jnp.dot(
        jnp.concatenate(shifted, axis=1), weight[...], preferred_element_type=jnp.float32
    ).reshape(strip + 2, columns, 3 * channels)
    total = centre[pl.ds(step * strip, strip)]
    for a in range(3):
        total = total + taps[a : a + strip, :, a * channels : (a + 1) * channels]
    out[...] = total.astype(out.dtype)


def convolve(pair_two, mirrored, valid_i, valid_j, halos, weight):
    rows, columns, channels = pair_two.shape
    strip = math.gcd(32, rows)
    operands = [pair_two, *[a for part in mirrored for a in part], valid_j, *halos, weight]
    fixed = lambda a: pl.BlockSpec(a.shape, lambda n, rank=a.ndim: (0,) * rank)
    return pl.pallas_call(
        functools.partial(conv_kernel, parts=[tuple(range(len(part))) for part in mirrored]),
        grid=(rows // strip,),
        in_specs=[pl.BlockSpec(memory_space=pltpu.SMEM)] + [fixed(a) for a in operands],
        out_specs=pl.BlockSpec((strip, columns, channels), lambda n: (n, 0, 0)),
        out_shape=jax.ShapeDtypeStruct(pair_two.shape, jnp.bfloat16),
        scratch_shapes=[
            pltpu.VMEM((rows + 2, columns + 16, channels), jnp.float32),
            pltpu.VMEM((rows, columns, channels), jnp.float32),
        ],
        compiler_params=kernel_params(40),
        cost_estimate=pl.CostEstimate(
            flops=18 * rows * columns * channels * channels,
            bytes_accessed=3 << 20,
            transcendentals=0,
        ),
    )(valid_i, *operands)


def shifts(size, step):
    return [(n, (n + step) % size) for n in range(size)]


def on_device(
    pair_input,
    alignment_features,
    alignment_mask,
    token_valid,
    left_weight,
    right_weight,
    output_weight,
    gate_weight,
    up_weight,
    down_weight,
    kernel_weight,
):
    rows_dev, cols_dev, channels = pair_input.shape
    local_rows, local_tokens, align_width = alignment_features.shape
    width = left_weight.shape[1]
    row_count, col_count = lax.axis_size("row"), lax.axis_size(plane)
    x_count, core_count = lax.axis_size("col"), lax.axis_size("chan")
    row_index, col_index = lax.axis_index("row"), lax.axis_index(plane)
    x_index, core_index = lax.axis_index("col"), lax.axis_index("chan")
    square = row_count == col_count
    tiles = [(r, c) for r in range(row_count) for c in range(col_count)]
    place_of = lambda r, c: r * col_count + c

    flat = alignment_features.reshape(local_rows * local_tokens, align_width)
    mask_rows = alignment_mask.astype(jnp.float32)

    def project(flat, weight):
        value = jnp.dot(flat, weight, preferred_element_type=jnp.float32)
        value = value.reshape(local_rows, local_tokens, width) * mask_rows[:, :, None]
        return value.astype(jnp.bfloat16)

    narrow_mask = alignment_mask.astype(jnp.bfloat16)

    def beside(side, mask):
        depth, tokens = mask.shape
        room = jnp.pad(mask, ((0, 0), (0, lanes - tokens % lanes)))
        return jnp.concatenate([side.reshape(depth, tokens * width), room], axis=1)

    if square:
        left_block = beside(project(flat, left_weight), narrow_mask)
        flat, left_block = lax.optimization_barrier((flat, left_block))
        mirror_pairs = [(place_of(r, c), place_of(c, r)) for r, c in tiles]
        first = lax.ppermute(left_block, whole, mirror_pairs)
        right_block = beside(project(flat, right_weight), narrow_mask)
        col_side, col_places = [right_block], [row_index]
        for step in range(1, row_count):
            col_side.append(lax.ppermute(right_block, "row", shifts(row_count, -step)))
            col_places.append((row_index + step) % row_count)
        row_side, row_places = [first], [col_index]
        for step in range(1, x_count):
            row_side.append(lax.ppermute(first, "col", shifts(x_count, -step)))
            row_places.append(((x_index + step) % x_count) * core_count + core_index)
        for step in range(1, core_count):
            for n in range(x_count):
                row_side.append(lax.ppermute(row_side[n], "chan", shifts(core_count, -step)))
                row_places.append(
                    ((x_index + n) % x_count) * core_count + (core_index + step) % core_count
                )
        places = jnp.stack(row_places + col_places).astype(jnp.int32) * local_rows
    else:
        left_wide = lax.all_gather(project(flat, left_weight), plane, axis=1, tiled=True)
        mask_wide = lax.all_gather(narrow_mask, plane, axis=1, tiled=True)
        turn = lambda a: lax.all_to_all(a, "row", split_axis=1, concat_axis=0, tiled=True)
        gather = lambda a: lax.all_gather(a, "row", axis=0, tiled=True)
        row_side = [beside(turn(left_wide), turn(mask_wide))]
        col_side = [beside(gather(project(flat, right_weight)), gather(narrow_mask))]
        places = jnp.zeros((2,), jnp.int32)

    split = output_weight.reshape(width // turns, turns, width, channels)
    weight = jnp.stack(
        [jnp.roll(split, u, axis=1).reshape(width * width, channels) for u in range(turns)]
    )
    gate_up = jnp.concatenate([gate_weight * 0.5, up_weight], axis=1).astype(jnp.bfloat16)
    conv_weight = kernel_weight.transpose(1, 2, 0, 3).reshape(3 * channels, 3 * channels)
    base = jnp.swapaxes(pair_input, 0, 1)

    sides = arrange(places, row_side, col_side, width, rows_dev, cols_dev)

    def run(first, count, strip, after=None):
        row_channels = sides[0]
        if after is not None:
            row_channels, _ = lax.optimization_barrier((row_channels, after))
        return tile_strips(
            first, count, strip, row_channels, *sides[1:], base, weight, gate_up, down_weight
        )

    ahead = lambda size: [(n, n + 1) for n in range(size - 1)]
    back = lambda size: [(n + 1, n) for n in range(size - 1)]

    if square and cols_dev % (8 * unit) == 0 and x_count > 1:
        part = cols_dev // 8
        host = lambda r, c: place_of(r, (r // core_count) * core_count + c % core_count)
        away = [(r, c) for r, c in tiles if r // core_count != c // core_count]
        near = [(r, c) for r, c in tiles if r // core_count == c // core_count]
        to_host = [(place_of(r, c), host(r, c)) for r, c in away]
        from_host = [(host(r, c), place_of(c, r)) for r, c in away]
        beside_pairs = [(place_of(r, c), place_of(c, r)) for r, c in near]
        send = lambda value, pairs: lax.ppermute(value, whole, pairs)
        last = run(6 * part, 2 * part, 2 * part)
        mirrored_last = send(last, mirror_pairs)
        opening = run(0, 3 * part, 3 * part, last)
        hosted = send(opening, to_host)
        mirrored_near = send(opening, beside_pairs)
        middle = run(3 * part, 3 * part, 3 * part, opening)
        mirrored_middle = send(middle, mirror_pairs)
        mirrored_away = send(hosted, from_host)
        turned = jnp.concatenate([opening, middle, last], axis=0)
        turned, _ = lax.optimization_barrier((turned, hosted))
        edges = jnp.stack([turned[0], turned[-1], turned[:, 0], turned[:, -1]])
        edges = send(edges, mirror_pairs)
        mirrored = [[mirrored_away, mirrored_near], [mirrored_middle], [mirrored_last]]
    else:
        turned = run(0, cols_dev, math.gcd(unit, cols_dev))
        share = rows_dev // col_count
        fold = row_count // col_count
        second = lax.all_to_all(
            lax.all_to_all(
                jnp.swapaxes(turned, 0, 1), plane, split_axis=0, concat_axis=1, tiled=True
            ),
            "row",
            split_axis=1,
            concat_axis=0,
            tiled=True,
        )
        third = lax.all_to_all(
            jnp.swapaxes(second, 0, 1), plane, split_axis=1, concat_axis=1, tiled=True
        )
        full = (
            third.reshape(rows_dev, col_count, fold, share, channels)
            .transpose(0, 2, 1, 3, 4)
            .reshape(rows_dev, cols_dev, channels)
        )
        mirrored = [[full]]
        edges = (full[0], full[-1], full[:, 0], full[:, -1])

    pair_two = jnp.swapaxes(turned, 0, 1)
    valid_i = lax.dynamic_slice_in_dim(token_valid, row_index * rows_dev, rows_dev)
    valid_j = lax.dynamic_slice_in_dim(token_valid, col_index * cols_dev, cols_dev)
    keep_i = valid_i.astype(jnp.float32)[:, None]
    keep_j = valid_j.astype(jnp.float32)[:, None]
    mean = lambda a, b: (a.astype(jnp.float32) + b.astype(jnp.float32)) * 0.5
    last_i, last_j = rows_dev - 1, cols_dev - 1
    first_line = (mean(turned[:, 0], edges[0]) * keep_j * keep_i[0]).astype(jnp.bfloat16)
    last_line = (mean(turned[:, -1], edges[1]) * keep_j * keep_i[last_i]).astype(jnp.bfloat16)
    first_side = (mean(turned[0], edges[2]) * keep_i * keep_j[0]).astype(jnp.bfloat16)
    last_side = (mean(turned[-1], edges[3]) * keep_i * keep_j[last_j]).astype(jnp.bfloat16)
    left = lax.ppermute(last_side, plane, ahead(col_count))
    right = lax.ppermute(first_side, plane, back(col_count))
    top = lax.ppermute(last_line, "row", ahead(row_count))
    bottom = lax.ppermute(first_line, "row", back(row_count))

    def corner(value, down, across):
        pairs = [
            (place_of(r, c), place_of(r + down, c + across))
            for r, c in tiles
            if 0 <= r + down < row_count and 0 <= c + across < col_count
        ]
        return lax.ppermute(jnp.broadcast_to(value, (16, channels)), whole, pairs)[:1]

    top_left = corner(last_line[-1:], 1, 1)
    top_right = corner(last_line[:1], 1, -1)
    bottom_left = corner(first_line[-1:], -1, 1)
    bottom_right = corner(first_line[:1], -1, -1)
    left = jnp.concatenate([top_left, left, bottom_left], axis=0)
    right = jnp.concatenate([top_right, right, bottom_right], axis=0)
    wide_valid = jnp.broadcast_to(keep_j, (cols_dev, channels))
    return convolve(
        pair_two,
        mirrored,
        valid_i,
        wide_valid,
        [top, bottom, left, right],
        conv_weight,
    )


def solution(mesh):
    placed = (
        P(("groups", "row"), plane, None),
        P("row", ("groups", "col", "chan"), None),
        P("row", ("groups", "col", "chan")),
        P("groups"),
        P(),
        P(),
        P(),
        P(),
        P(),
        P(),
        P(),
    )
    return jax.shard_map(
        on_device,
        mesh=mesh,
        in_specs=placed,
        out_specs=P(("groups", "row"), plane, None),
        check_vma=False,
    )
```

```python
import functools
import math

import jax
import jax.numpy as jnp
from jax import lax
from jax.experimental import pallas as pl
from jax.experimental.pallas import tpu as pltpu
from jax.sharding import PartitionSpec as P

epsilon = 1e-05
lanes = 128
turns = 4
plane = ("col", "chan")
whole = ("row", "col", "chan")
unit = 8


def kernel_params(mib):
    return pltpu.CompilerParams(vmem_limit_bytes=mib * 1024 * 1024)


def arrange_kernel(
    places, *refs, row_blocks, col_blocks, width, tokens_row, tokens_col
):
    row_refs, refs = refs[:row_blocks], refs[row_blocks:]
    col_refs, refs = refs[:col_blocks], refs[col_blocks:]
    row_side, lane_side, scale, gathered, turned, row_mask, col_mask = refs
    high = width // turns
    row_span, col_span = tokens_row * width, tokens_col * width
    for n, block in enumerate(row_refs):
        at = pl.ds(pl.multiple_of(places[n], 16), block.shape[0])
        gathered[at, :] = block[:, :row_span]
        row_mask[at, :] = block[:, row_span:]
    for n, block in enumerate(col_refs):
        at = pl.ds(pl.multiple_of(places[row_blocks + n], 16), block.shape[0])
        col_mask[at, :] = block[:, col_span:]
        for g in range(col_span // lanes):
            spot = slice(g * lanes, (g + 1) * lanes)
            piece = block[:, spot]
            lane_side[0, at, spot] = piece
            piece = piece.astype(jnp.float32)
            for turn in range(1, turns):
                lane_side[turn, at, spot] = pltpu.roll(piece, turn * width, 1).astype(jnp.bfloat16)
    for n in range(row_span // lanes):
        spot = slice(n * lanes, (n + 1) * lanes)
        turned[spot, :] = gathered[:, spot].astype(jnp.float32).T
    for channel in range(width):
        spot = ((channel % turns) * high + channel // turns) * tokens_row
        rows = turned[pl.ds(channel, tokens_row, stride=width), :]
        row_side[spot : spot + tokens_row, :] = rows.astype(jnp.bfloat16)
    counts = lax.dot_general(
        row_mask[...],
        col_mask[...],
        (((0,), (0,)), ((), ())),
        preferred_element_type=jnp.float32,
    )[:tokens_row]
    inverse = 1.0 / jnp.maximum(counts, 1.0)
    strip = scale.shape[0]
    for n in range(strip):
        count = tokens_col // strip
        scale[n, :, :count] = inverse[:, n * count : (n + 1) * count]


def arrange(places, row_side, col_side, width, tokens_row, tokens_col):
    depth = sum(block.shape[0] for block in row_side)
    body = functools.partial(
        arrange_kernel,
        row_blocks=len(row_side),
        col_blocks=len(col_side),
        width=width,
        tokens_row=tokens_row,
        tokens_col=tokens_col,
    )
    in_vmem = pl.BlockSpec(memory_space=pltpu.VMEM)
    return pl.pallas_call(
        body,
        in_specs=[pl.BlockSpec(memory_space=pltpu.SMEM)]
        + [in_vmem] * (len(row_side) + len(col_side)),
        out_specs=[in_vmem] * 3,
        out_shape=[
            jax.ShapeDtypeStruct((tokens_row * width, depth), jnp.bfloat16),
            jax.ShapeDtypeStruct((turns, depth, tokens_col * width), jnp.bfloat16),
            jax.ShapeDtypeStruct((tokens_col // unit, tokens_row, lanes), jnp.float32),
        ],
        scratch_shapes=[
            pltpu.VMEM((depth, tokens_row * width), jnp.bfloat16),
            pltpu.VMEM((tokens_row * width, depth), jnp.float32),
            pltpu.VMEM((depth, lanes), jnp.bfloat16),
            pltpu.VMEM((depth, lanes), jnp.bfloat16),
        ],
        compiler_params=kernel_params(12),
        cost_estimate=pl.CostEstimate(flops=1024, bytes_accessed=1024, transcendentals=0),
    )(places, *row_side, *col_side)


def transition_rows(values, gate_up, down):
    channels = values.shape[1]
    mean_of = jnp.full((channels, channels), 1.0 / channels, jnp.bfloat16)
    centre = jnp.dot(values.astype(jnp.bfloat16), mean_of, preferred_element_type=jnp.float32)
    offset = values - centre
    squares = (offset * offset).astype(jnp.bfloat16)
    spread = jnp.dot(squares, mean_of, preferred_element_type=jnp.float32)
    normed = (offset * lax.rsqrt(spread + epsilon)).astype(jnp.bfloat16)
    both = jnp.dot(normed, gate_up, preferred_element_type=jnp.float32)
    hidden_width = gate_up.shape[1] // 2
    half, up = both[:, :hidden_width], both[:, hidden_width:]
    hidden = ((half + half * jnp.tanh(half)) * up).astype(jnp.bfloat16)
    return values + jnp.dot(hidden, down, preferred_element_type=jnp.float32)


def tile_kernel(
    row_side, lane_side, scale, base, weight, gate_up, down, out, products, stacked, held
):
    strip, tokens_row, channels = out.shape
    width = lane_side.shape[2] // strip
    high = width // turns
    groups = strip // turns
    span = high * tokens_row
    for turn in range(turns):
        products[turn] = jnp.dot(
            row_side[turn * span : (turn + 1) * span, :],
            lane_side[turn],
            preferred_element_type=jnp.float32,
        ).astype(jnp.bfloat16)
    position = lax.broadcasted_iota(jnp.int32, (tokens_row, lanes), 1) // width
    for g in range(groups):
        for h in range(high):
            parts = [
                products[t, h * tokens_row : (h + 1) * tokens_row, g * lanes : (g + 1) * lanes]
                for t in range(turns)
            ]
            for u in range(turns):
                mixed = parts[(turns - 1 - u) % turns]
                for t in range(turns - 1):
                    mixed = jnp.where(position == t, parts[(t - u) % turns], mixed)
                stacked[
                    u, g * tokens_row : (g + 1) * tokens_row, h * lanes : (h + 1) * lanes
                ] = mixed
    for u in range(turns):
        update = jnp.dot(stacked[u], weight[u], preferred_element_type=jnp.float32)
        for g in range(groups):
            n = turns * g + u
            factor = scale[n // unit][:, n % unit : n % unit + 1]
            value = update[g * tokens_row : (g + 1) * tokens_row] * factor
            value = base[n].astype(jnp.float32) + value
            held[n * tokens_row : (n + 1) * tokens_row, :] = value.astype(jnp.bfloat16)
    piece = math.gcd(strip, 24) if strip > 24 else strip
    for first in range(0, strip, piece):
        at = slice(first * tokens_row, (first + piece) * tokens_row)
        result = transition_rows(held[at, :].astype(jnp.float32), gate_up[...], down[...])
        out[first : first + piece] = result.astype(out.dtype).reshape(piece, tokens_row, channels)


def tile_strips(first, count, strip, row_side, lane_side, scale, base, weight, gate_up, down):
    tokens_row, channels = base.shape[1:]
    turn_count, depth, span = lane_side.shape
    width = span // base.shape[0]
    start = first // strip
    fixed = lambda a: pl.BlockSpec(a.shape, lambda n, rank=a.ndim: (0,) * rank)
    return pl.pallas_call(
        tile_kernel,
        grid=(count // strip,),
        in_specs=[
            fixed(row_side),
            pl.BlockSpec((turn_count, depth, strip * width), lambda n: (0, 0, n + start)),
            pl.BlockSpec((strip // unit, tokens_row, lanes), lambda n: (n + start, 0, 0)),
            pl.BlockSpec((strip, tokens_row, channels), lambda n: (n + start, 0, 0)),
            fixed(weight),
            fixed(gate_up),
            fixed(down),
        ],
        out_specs=pl.BlockSpec((strip, tokens_row, channels), lambda n: (n, 0, 0)),
        out_shape=jax.ShapeDtypeStruct((count, tokens_row, channels), jnp.bfloat16),
        scratch_shapes=[
            pltpu.VMEM((turns, tokens_row * width // turns, strip * width), jnp.bfloat16),
            pltpu.VMEM((turns, strip // turns * tokens_row, width * width), jnp.bfloat16),
            pltpu.VMEM((strip * tokens_row, channels), jnp.bfloat16),
        ],
        compiler_params=kernel_params(40),
        cost_estimate=pl.CostEstimate(flops=1024, bytes_accessed=1024, transcendentals=0),
    )(row_side, lane_side, scale, base, weight, gate_up, down)


def conv_kernel(
    valid_i, pair_two, *refs, parts
):
    counts = [len(p) for p in parts]
    total_parts = sum(counts)
    mirrored, refs = refs[:total_parts], refs[total_parts:]
    valid_j, top, bottom, left, right, weight, out, padded, centre = refs
    step = pl.program_id(0)
    rows, columns, channels = pair_two.shape
    strip = out.shape[0]

    @pl.when(step == 0)
    def _():
        padded[0, 8 : 8 + columns, :] = top[...].astype(jnp.float32)
        padded[rows + 1, 8 : 8 + columns, :] = bottom[...].astype(jnp.float32)
        i = 0
        used = 0
        for count in counts:
            group = mirrored[used : used + count]
            used += count
            for n in range(group[0].shape[0]):
                other = group[0][n].astype(jnp.float32)
                for more in group[1:]:
                    other = other + more[n].astype(jnp.float32)
                symmetric = (pair_two[i].astype(jnp.float32) + other) * 0.5
                centre[i] = symmetric
                keep = valid_j[...] * valid_i[i].astype(jnp.float32)
                padded[i + 1, 8 : 8 + columns, :] = symmetric * keep
                i += 1
        for i in range(rows + 2):
            padded[i, 7:8, :] = left[i : i + 1, :].astype(jnp.float32)
            padded[i, 8 + columns : 9 + columns, :] = right[i : i + 1, :].astype(jnp.float32)

    window = padded.at[pl.ds(step * strip, strip + 2)]
    shifted = [
        window[:, 7 + b : 7 + b + columns, :]
        .astype(jnp.bfloat16)
        .reshape((strip + 2) * columns, channels)
        for b in range(3)
    ]
    taps = jnp.dot(
        jnp.concatenate(shifted, axis=1), weight[...], preferred_element_type=jnp.float32
    ).reshape(strip + 2, columns, 3 * channels)
    total = centre[pl.ds(step * strip, strip)]
    for a in range(3):
        total = total + taps[a : a + strip, :, a * channels : (a + 1) * channels]
    out[...] = total.astype(out.dtype)


def convolve(pair_two, mirrored, valid_i, valid_j, halos, weight):
    rows, columns, channels = pair_two.shape
    strip = math.gcd(32, rows)
    operands = [pair_two, *[a for part in mirrored for a in part], valid_j, *halos, weight]
    fixed = lambda a: pl.BlockSpec(a.shape, lambda n, rank=a.ndim: (0,) * rank)
    return pl.pallas_call(
        functools.partial(conv_kernel, parts=[tuple(range(len(part))) for part in mirrored]),
        grid=(rows // strip,),
        in_specs=[pl.BlockSpec(memory_space=pltpu.SMEM)] + [fixed(a) for a in operands],
        out_specs=pl.BlockSpec((strip, columns, channels), lambda n: (n, 0, 0)),
        out_shape=jax.ShapeDtypeStruct(pair_two.shape, jnp.bfloat16),
        scratch_shapes=[
            pltpu.VMEM((rows + 2, columns + 16, channels), jnp.float32),
            pltpu.VMEM((rows, columns, channels), jnp.float32),
        ],
        compiler_params=kernel_params(40),
        cost_estimate=pl.CostEstimate(
            flops=18 * rows * columns * channels * channels,
            bytes_accessed=3 << 20,
            transcendentals=0,
        ),
    )(valid_i, *operands)


def shifts(size, step):
    return [(n, (n + step) % size) for n in range(size)]


def on_device(
    pair_input,
    alignment_features,
    alignment_mask,
    token_valid,
    left_weight,
    right_weight,
    output_weight,
    gate_weight,
    up_weight,
    down_weight,
    kernel_weight,
):
    rows_dev, cols_dev, channels = pair_input.shape
    local_rows, local_tokens, align_width = alignment_features.shape
    width = left_weight.shape[1]
    row_count, col_count = lax.axis_size("row"), lax.axis_size(plane)
    x_count, core_count = lax.axis_size("col"), lax.axis_size("chan")
    row_index, col_index = lax.axis_index("row"), lax.axis_index(plane)
    x_index, core_index = lax.axis_index("col"), lax.axis_index("chan")
    square = row_count == col_count
    tiles = [(r, c) for r in range(row_count) for c in range(col_count)]
    place_of = lambda r, c: r * col_count + c

    flat = alignment_features.reshape(local_rows * local_tokens, align_width)
    mask_rows = alignment_mask.astype(jnp.float32)

    def project(flat, weight):
        value = jnp.dot(flat, weight, preferred_element_type=jnp.float32)
        value = value.reshape(local_rows, local_tokens, width) * mask_rows[:, :, None]
        return value.astype(jnp.bfloat16)

    narrow_mask = alignment_mask.astype(jnp.bfloat16)

    def beside(side, mask):
        depth, tokens = mask.shape
        room = jnp.pad(mask, ((0, 0), (0, lanes - tokens % lanes)))
        return jnp.concatenate([side.reshape(depth, tokens * width), room], axis=1)

    if square:
        left_block = beside(project(flat, left_weight), narrow_mask)
        flat, left_block = lax.optimization_barrier((flat, left_block))
        mirror_pairs = [(place_of(r, c), place_of(c, r)) for r, c in tiles]
        first = lax.ppermute(left_block, whole, mirror_pairs)
        right_block = beside(project(flat, right_weight), narrow_mask)
        col_side, col_places = [right_block], [row_index]
        for step in range(1, row_count):
            col_side.append(lax.ppermute(right_block, "row", shifts(row_count, -step)))
            col_places.append((row_index + step) % row_count)
        row_side, row_places = [first], [col_index]
        for step in range(1, x_count):
            row_side.append(lax.ppermute(first, "col", shifts(x_count, -step)))
            row_places.append(((x_index + step) % x_count) * core_count + core_index)
        for step in range(1, core_count):
            for n in range(x_count):
                row_side.append(lax.ppermute(row_side[n], "chan", shifts(core_count, -step)))
                row_places.append(
                    ((x_index + n) % x_count) * core_count + (core_index + step) % core_count
                )
        places = jnp.stack(row_places + col_places).astype(jnp.int32) * local_rows
    else:
        left_wide = lax.all_gather(project(flat, left_weight), plane, axis=1, tiled=True)
        mask_wide = lax.all_gather(narrow_mask, plane, axis=1, tiled=True)
        turn = lambda a: lax.all_to_all(a, "row", split_axis=1, concat_axis=0, tiled=True)
        gather = lambda a: lax.all_gather(a, "row", axis=0, tiled=True)
        row_side = [beside(turn(left_wide), turn(mask_wide))]
        col_side = [beside(gather(project(flat, right_weight)), gather(narrow_mask))]
        places = jnp.zeros((2,), jnp.int32)

    split = output_weight.reshape(width // turns, turns, width, channels)
    weight = jnp.stack(
        [jnp.roll(split, u, axis=1).reshape(width * width, channels) for u in range(turns)]
    )
    gate_up = jnp.concatenate([gate_weight * 0.5, up_weight], axis=1).astype(jnp.bfloat16)
    conv_weight = kernel_weight.transpose(1, 2, 0, 3).reshape(3 * channels, 3 * channels)
    base = jnp.swapaxes(pair_input, 0, 1)

    sides = arrange(places, row_side, col_side, width, rows_dev, cols_dev)

    def run(first, count, strip, after=None):
        row_channels = sides[0]
        if after is not None:
            row_channels, _ = lax.optimization_barrier((row_channels, after))
        return tile_strips(
            first, count, strip, row_channels, *sides[1:], base, weight, gate_up, down_weight
        )

    ahead = lambda size: [(n, n + 1) for n in range(size - 1)]
    back = lambda size: [(n + 1, n) for n in range(size - 1)]

    if square and cols_dev % (8 * unit) == 0 and x_count > 1:
        part = cols_dev // 8
        host = lambda r, c: place_of(r, (r // core_count) * core_count + c % core_count)
        away = [(r, c) for r, c in tiles if r // core_count != c // core_count]
        near = [(r, c) for r, c in tiles if r // core_count == c // core_count]
        to_host = [(place_of(r, c), host(r, c)) for r, c in away]
        from_host = [(host(r, c), place_of(c, r)) for r, c in away]
        beside_pairs = [(place_of(r, c), place_of(c, r)) for r, c in near]
        send = lambda value, pairs: lax.ppermute(value, whole, pairs)
        last = run(6 * part, 2 * part, 2 * part)
        mirrored_last = send(last, mirror_pairs)
        opening = run(0, 3 * part, 3 * part, last)
        hosted = send(opening, to_host)
        mirrored_near = send(opening, beside_pairs)
        middle = run(3 * part, 3 * part, 3 * part, opening)
        mirrored_middle = send(middle, mirror_pairs)
        mirrored_away = send(hosted, from_host)
        turned = jnp.concatenate([opening, middle, last], axis=0)
        mirrored = [[mirrored_away, mirrored_near], [mirrored_middle], [mirrored_last]]
    else:
        turned = run(0, cols_dev, math.gcd(unit, cols_dev))
        share = rows_dev // col_count
        fold = row_count // col_count
        second = lax.all_to_all(
            lax.all_to_all(
                jnp.swapaxes(turned, 0, 1), plane, split_axis=0, concat_axis=1, tiled=True
            ),
            "row",
            split_axis=1,
            concat_axis=0,
            tiled=True,
        )
        third = lax.all_to_all(
            jnp.swapaxes(second, 0, 1), plane, split_axis=1, concat_axis=1, tiled=True
        )
        full = (
            third.reshape(rows_dev, col_count, fold, share, channels)
            .transpose(0, 2, 1, 3, 4)
            .reshape(rows_dev, cols_dev, channels)
        )
        mirrored = [[full]]

    pair_two = jnp.swapaxes(turned, 0, 1)
    valid_i = lax.dynamic_slice_in_dim(token_valid, row_index * rows_dev, rows_dev)
    valid_j = lax.dynamic_slice_in_dim(token_valid, col_index * cols_dev, cols_dev)
    keep_i = valid_i.astype(jnp.float32)[:, None]
    keep_j = valid_j.astype(jnp.float32)[:, None]
    last_i, last_j = rows_dev - 1, cols_dev - 1
    parts = [[a.astype(jnp.float32) for a in part] for part in mirrored]
    along = lambda pick: jnp.concatenate([sum(pick(a) for a in part) for part in parts], axis=0)

    def edge(own, other, keep):
        return ((own.astype(jnp.float32) + other) * 0.5 * keep).astype(jnp.bfloat16)

    first_line = edge(turned[:, 0], sum(a[0] for a in parts[0]), keep_j * keep_i[0])
    last_line = edge(turned[:, -1], sum(a[-1] for a in parts[-1]), keep_j * keep_i[last_i])
    first_side = edge(turned[0], along(lambda a: a[:, 0]), keep_i * keep_j[0])
    last_side = edge(turned[-1], along(lambda a: a[:, -1]), keep_i * keep_j[last_j])
    left = lax.ppermute(last_side, plane, ahead(col_count))
    right = lax.ppermute(first_side, plane, back(col_count))
    border = lambda i, line: jnp.concatenate([left[i][None], line, right[i][None]], axis=0)
    top = lax.ppermute(border(last_i, last_line), "row", ahead(row_count))
    bottom = lax.ppermute(border(0, first_line), "row", back(row_count))
    left = jnp.concatenate([top[:1], left, bottom[:1]], axis=0)
    right = jnp.concatenate([top[-1:], right, bottom[-1:]], axis=0)
    wide_valid = jnp.broadcast_to(keep_j, (cols_dev, channels))
    return convolve(
        pair_two,
        mirrored,
        valid_i,
        wide_valid,
        [top[1:-1], bottom[1:-1], left, right],
        conv_weight,
    )


def solution(mesh):
    placed = (
        P(("groups", "row"), plane, None),
        P("row", ("groups", "col", "chan"), None),
        P("row", ("groups", "col", "chan")),
        P("groups"),
        P(),
        P(),
        P(),
        P(),
        P(),
        P(),
        P(),
    )
    return jax.shard_map(
        on_device,
        mesh=mesh,
        in_specs=placed,
        out_specs=P(("groups", "row"), plane, None),
        check_vma=False,
    )
```

```python
import functools
import math

import jax
import jax.numpy as jnp
from jax import lax
from jax.experimental import pallas as pl
from jax.experimental.pallas import tpu as pltpu
from jax.sharding import PartitionSpec as P

epsilon = 1e-05
lanes = 128
turns = 4
plane = ("col", "chan")
whole = ("row", "col", "chan")
unit = 8


def kernel_params(mib):
    return pltpu.CompilerParams(vmem_limit_bytes=mib * 1024 * 1024)


def project_kernel(features, mask, left_weight, right_weight, left, right):
    depth, tokens = mask.shape
    inner, width = left_weight.shape
    group = lanes // width

    def chosen(rows, columns, test):
        a = lax.broadcasted_iota(jnp.int32, (rows, columns), 0)
        b = lax.broadcasted_iota(jnp.int32, (rows, columns), 1)
        return jnp.where(test(a, b), 1.0, 0.0).astype(jnp.bfloat16)

    dot = lambda a, b: jnp.dot(a, b, preferred_element_type=jnp.float32)
    repeat_rows = chosen(group * inner, inner, lambda a, b: a % inner == b)
    repeat_lanes = chosen(width, lanes, lambda a, b: a == b % width)
    own_block = chosen(group * inner, lanes, lambda a, b: a // inner == b // width)
    spread = []
    for weight in (left_weight, right_weight):
        tall = dot(repeat_rows, weight[...]).astype(jnp.bfloat16)
        spread.append(dot(tall, repeat_lanes).astype(jnp.bfloat16) * own_block)
    both = jnp.concatenate(spread, axis=1)
    kept = mask[...].astype(jnp.float32).astype(jnp.bfloat16)
    wide_mask = dot(kept, chosen(tokens, tokens * width, lambda a, b: a == b // width))
    for g in range(tokens // group):
        at = slice(g * lanes, (g + 1) * lanes)
        value = dot(features[:, g * group * inner : (g + 1) * group * inner], both)
        left[:, at] = (value[:, :lanes] * wide_mask[:, at]).astype(jnp.bfloat16)
        right[:, at] = (value[:, lanes:] * wide_mask[:, at]).astype(jnp.bfloat16)
    narrow = dot(kept, chosen(tokens, lanes, lambda a, b: a == b)).astype(jnp.bfloat16)
    left[:, tokens * width :] = narrow
    right[:, tokens * width :] = narrow


def project_sides(features, mask, left_weight, right_weight):
    depth, tokens = mask.shape
    span = tokens * left_weight.shape[1] + lanes
    in_vmem = pl.BlockSpec(memory_space=pltpu.VMEM)
    return pl.pallas_call(
        project_kernel,
        in_specs=[in_vmem] * 4,
        out_specs=[in_vmem] * 2,
        out_shape=[jax.ShapeDtypeStruct((depth, span), jnp.bfloat16)] * 2,
        compiler_params=kernel_params(8),
        cost_estimate=pl.CostEstimate(flops=1024, bytes_accessed=1024, transcendentals=0),
    )(features.reshape(depth, -1), mask, left_weight, right_weight)


def arrange_kernel(
    places, *refs, row_blocks, col_blocks, width, tokens_row, tokens_col
):
    row_refs, refs = refs[:row_blocks], refs[row_blocks:]
    col_refs, refs = refs[:col_blocks], refs[col_blocks:]
    row_side, lane_side, scale, gathered, turned, row_mask, col_mask = refs
    high = width // turns
    row_span, col_span = tokens_row * width, tokens_col * width
    for n, block in enumerate(row_refs):
        at = pl.ds(pl.multiple_of(places[n], 16), block.shape[0])
        gathered[at, :] = block[:, :row_span]
        row_mask[at, :] = block[:, row_span:]
    for n, block in enumerate(col_refs):
        at = pl.ds(pl.multiple_of(places[row_blocks + n], 16), block.shape[0])
        col_mask[at, :] = block[:, col_span:]
        for g in range(col_span // lanes):
            spot = slice(g * lanes, (g + 1) * lanes)
            piece = block[:, spot]
            lane_side[0, at, spot] = piece
            piece = piece.astype(jnp.float32)
            for turn in range(1, turns):
                lane_side[turn, at, spot] = pltpu.roll(piece, turn * width, 1).astype(jnp.bfloat16)
    for n in range(row_span // lanes):
        spot = slice(n * lanes, (n + 1) * lanes)
        turned[spot, :] = gathered[:, spot].astype(jnp.float32).T
    for channel in range(width):
        spot = ((channel % turns) * high + channel // turns) * tokens_row
        rows = turned[pl.ds(channel, tokens_row, stride=width), :]
        row_side[spot : spot + tokens_row, :] = rows.astype(jnp.bfloat16)
    counts = lax.dot_general(
        row_mask[...],
        col_mask[...],
        (((0,), (0,)), ((), ())),
        preferred_element_type=jnp.float32,
    )[:tokens_row]
    inverse = 1.0 / jnp.maximum(counts, 1.0)
    strip = scale.shape[0]
    for n in range(strip):
        count = tokens_col // strip
        scale[n, :, :count] = inverse[:, n * count : (n + 1) * count]


def arrange(places, row_side, col_side, width, tokens_row, tokens_col):
    depth = sum(block.shape[0] for block in row_side)
    body = functools.partial(
        arrange_kernel,
        row_blocks=len(row_side),
        col_blocks=len(col_side),
        width=width,
        tokens_row=tokens_row,
        tokens_col=tokens_col,
    )
    in_vmem = pl.BlockSpec(memory_space=pltpu.VMEM)
    return pl.pallas_call(
        body,
        in_specs=[pl.BlockSpec(memory_space=pltpu.SMEM)]
        + [in_vmem] * (len(row_side) + len(col_side)),
        out_specs=[in_vmem] * 3,
        out_shape=[
            jax.ShapeDtypeStruct((tokens_row * width, depth), jnp.bfloat16),
            jax.ShapeDtypeStruct((turns, depth, tokens_col * width), jnp.bfloat16),
            jax.ShapeDtypeStruct((tokens_col // unit, tokens_row, lanes), jnp.float32),
        ],
        scratch_shapes=[
            pltpu.VMEM((depth, tokens_row * width), jnp.bfloat16),
            pltpu.VMEM((tokens_row * width, depth), jnp.float32),
            pltpu.VMEM((depth, lanes), jnp.bfloat16),
            pltpu.VMEM((depth, lanes), jnp.bfloat16),
        ],
        compiler_params=kernel_params(12),
        cost_estimate=pl.CostEstimate(flops=1024, bytes_accessed=1024, transcendentals=0),
    )(places, *row_side, *col_side)


def transition_rows(values, gate_up, down):
    channels = values.shape[1]
    mean_of = jnp.full((channels, channels), 1.0 / channels, jnp.bfloat16)
    centre = jnp.dot(values.astype(jnp.bfloat16), mean_of, preferred_element_type=jnp.float32)
    offset = values - centre
    squares = (offset * offset).astype(jnp.bfloat16)
    spread = jnp.dot(squares, mean_of, preferred_element_type=jnp.float32)
    normed = (offset * lax.rsqrt(spread + epsilon)).astype(jnp.bfloat16)
    both = jnp.dot(normed, gate_up, preferred_element_type=jnp.float32)
    hidden_width = gate_up.shape[1] // 2
    half, up = both[:, :hidden_width], both[:, hidden_width:]
    hidden = ((half + half * jnp.tanh(half)) * up).astype(jnp.bfloat16)
    return values + jnp.dot(hidden, down, preferred_element_type=jnp.float32)


def tile_kernel(
    row_side,
    lane_side,
    scale,
    base,
    weight,
    gate_up,
    down,
    out,
    products,
    stacked,
    held,
    *,
    first,
    width,
):
    strip, tokens_row, channels = out.shape
    high = width // turns
    groups = strip // turns
    span = high * tokens_row
    for turn in range(turns):
        products[turn] = jnp.dot(
            row_side[turn * span : (turn + 1) * span, :],
            lane_side[turn, :, first * width : (first + strip) * width],
            preferred_element_type=jnp.float32,
        ).astype(jnp.bfloat16)
    position = lax.broadcasted_iota(jnp.int32, (tokens_row, lanes), 1) // width
    for g in range(groups):
        for h in range(high):
            parts = [
                products[t, h * tokens_row : (h + 1) * tokens_row, g * lanes : (g + 1) * lanes]
                for t in range(turns)
            ]
            for u in range(turns):
                mixed = parts[(turns - 1 - u) % turns]
                for t in range(turns - 1):
                    mixed = jnp.where(position == t, parts[(t - u) % turns], mixed)
                stacked[
                    u, g * tokens_row : (g + 1) * tokens_row, h * lanes : (h + 1) * lanes
                ] = mixed
    for u in range(turns):
        update = jnp.dot(stacked[u], weight[u], preferred_element_type=jnp.float32)
        for g in range(groups):
            n = turns * g + u
            at = first + n
            factor = scale[at // unit][:, at % unit : at % unit + 1]
            value = update[g * tokens_row : (g + 1) * tokens_row] * factor
            value = base[at].astype(jnp.float32) + value
            held[n * tokens_row : (n + 1) * tokens_row, :] = value.astype(jnp.bfloat16)
    piece = strip if strip <= 32 else math.gcd(strip, 24)
    for start in range(0, strip, piece):
        at = slice(start * tokens_row, (start + piece) * tokens_row)
        result = transition_rows(held[at, :].astype(jnp.float32), gate_up[...], down[...])
        out[start : start + piece] = result.astype(out.dtype).reshape(piece, tokens_row, channels)


def tile_strip(first, strip, row_side, lane_side, scale, base, weight, gate_up, down):
    tokens_row, channels = base.shape[1:]
    width = lane_side.shape[2] // base.shape[0]
    operands = [row_side, lane_side, scale, base, weight, gate_up, down]
    in_vmem = pl.BlockSpec(memory_space=pltpu.VMEM)
    return pl.pallas_call(
        functools.partial(tile_kernel, first=first, width=width),
        in_specs=[in_vmem] * len(operands),
        out_specs=in_vmem,
        out_shape=jax.ShapeDtypeStruct((strip, tokens_row, channels), jnp.bfloat16),
        scratch_shapes=[
            pltpu.VMEM((turns, tokens_row * width // turns, strip * width), jnp.bfloat16),
            pltpu.VMEM((turns, strip // turns * tokens_row, width * width), jnp.bfloat16),
            pltpu.VMEM((strip * tokens_row, channels), jnp.bfloat16),
        ],
        compiler_params=kernel_params(40),
        cost_estimate=pl.CostEstimate(flops=1024, bytes_accessed=1024, transcendentals=0),
    )(*operands)


def conv_kernel(
    valid_i, pair_two, *refs, parts
):
    counts = [len(p) for p in parts]
    total_parts = sum(counts)
    mirrored, refs = refs[:total_parts], refs[total_parts:]
    valid_j, top, bottom, left, right, weight, out, padded, centre = refs
    step = pl.program_id(0)
    rows, columns, channels = pair_two.shape
    strip = out.shape[0]

    @pl.when(step == 0)
    def _():
        padded[0, 8 : 8 + columns, :] = top[...].astype(jnp.float32)
        padded[rows + 1, 8 : 8 + columns, :] = bottom[...].astype(jnp.float32)
        i = 0
        used = 0
        for count in counts:
            group = mirrored[used : used + count]
            used += count
            for n in range(group[0].shape[0]):
                other = group[0][n].astype(jnp.float32)
                for more in group[1:]:
                    other = other + more[n].astype(jnp.float32)
                symmetric = (pair_two[i].astype(jnp.float32) + other) * 0.5
                centre[i] = symmetric
                keep = valid_j[...] * valid_i[i].astype(jnp.float32)
                padded[i + 1, 8 : 8 + columns, :] = symmetric * keep
                i += 1
        for i in range(rows + 2):
            padded[i, 7:8, :] = left[i : i + 1, :].astype(jnp.float32)
            padded[i, 8 + columns : 9 + columns, :] = right[i : i + 1, :].astype(jnp.float32)

    window = padded.at[pl.ds(step * strip, strip + 2)]
    shifted = [
        window[:, 7 + b : 7 + b + columns, :]
        .astype(jnp.bfloat16)
        .reshape((strip + 2) * columns, channels)
        for b in range(3)
    ]
    taps = jnp.dot(
        jnp.concatenate(shifted, axis=1), weight[...], preferred_element_type=jnp.float32
    ).reshape(strip + 2, columns, 3 * channels)
    total = centre[pl.ds(step * strip, strip)]
    for a in range(3):
        total = total + taps[a : a + strip, :, a * channels : (a + 1) * channels]
    out[...] = total.astype(out.dtype)


def convolve(pair_two, mirrored, valid_i, valid_j, halos, weight):
    rows, columns, channels = pair_two.shape
    strip = math.gcd(32, rows)
    operands = [pair_two, *[a for part in mirrored for a in part], valid_j, *halos, weight]
    fixed = lambda a: pl.BlockSpec(a.shape, lambda n, rank=a.ndim: (0,) * rank)
    return pl.pallas_call(
        functools.partial(conv_kernel, parts=[tuple(range(len(part))) for part in mirrored]),
        grid=(rows // strip,),
        in_specs=[pl.BlockSpec(memory_space=pltpu.SMEM)] + [fixed(a) for a in operands],
        out_specs=pl.BlockSpec((strip, columns, channels), lambda n: (n, 0, 0)),
        out_shape=jax.ShapeDtypeStruct(pair_two.shape, jnp.bfloat16),
        scratch_shapes=[
            pltpu.VMEM((rows + 2, columns + 16, channels), jnp.float32),
            pltpu.VMEM((rows, columns, channels), jnp.float32),
        ],
        compiler_params=kernel_params(40),
        cost_estimate=pl.CostEstimate(
            flops=18 * rows * columns * channels * channels,
            bytes_accessed=3 << 20,
            transcendentals=0,
        ),
    )(valid_i, *operands)


def shifts(size, step):
    return [(n, (n + step) % size) for n in range(size)]


def on_device(
    pair_input,
    alignment_features,
    alignment_mask,
    token_valid,
    left_weight,
    right_weight,
    output_weight,
    gate_weight,
    up_weight,
    down_weight,
    kernel_weight,
):
    rows_dev, cols_dev, channels = pair_input.shape
    local_rows, local_tokens, align_width = alignment_features.shape
    width = left_weight.shape[1]
    row_count, col_count = lax.axis_size("row"), lax.axis_size(plane)
    x_count, core_count = lax.axis_size("col"), lax.axis_size("chan")
    row_index, col_index = lax.axis_index("row"), lax.axis_index(plane)
    x_index, core_index = lax.axis_index("col"), lax.axis_index("chan")
    square = row_count == col_count
    tiles = [(r, c) for r in range(row_count) for c in range(col_count)]
    place_of = lambda r, c: r * col_count + c

    flat = alignment_features.reshape(local_rows * local_tokens, align_width)
    mask_rows = alignment_mask.astype(jnp.float32)

    def project(flat, weight):
        value = jnp.dot(flat, weight, preferred_element_type=jnp.float32)
        value = value.reshape(local_rows, local_tokens, width) * mask_rows[:, :, None]
        return value.astype(jnp.bfloat16)

    narrow_mask = alignment_mask.astype(jnp.bfloat16)

    def beside(side, mask):
        depth, tokens = mask.shape
        room = jnp.pad(mask, ((0, 0), (0, lanes - tokens % lanes)))
        return jnp.concatenate([side.reshape(depth, tokens * width), room], axis=1)

    if square:
        left_block, right_block = project_sides(
            alignment_features, alignment_mask, left_weight, right_weight
        )
        mirror_pairs = [(place_of(r, c), place_of(c, r)) for r, c in tiles]
        first = lax.ppermute(left_block, whole, mirror_pairs)
        col_side, col_places = [right_block], [row_index]
        for step in range(1, row_count):
            col_side.append(lax.ppermute(right_block, "row", shifts(row_count, -step)))
            col_places.append((row_index + step) % row_count)
        row_side, row_places = [first], [col_index]
        for step in range(1, x_count):
            row_side.append(lax.ppermute(first, "col", shifts(x_count, -step)))
            row_places.append(((x_index + step) % x_count) * core_count + core_index)
        for step in range(1, core_count):
            for n in range(x_count):
                row_side.append(lax.ppermute(row_side[n], "chan", shifts(core_count, -step)))
                row_places.append(
                    ((x_index + n) % x_count) * core_count + (core_index + step) % core_count
                )
        places = jnp.stack(row_places + col_places).astype(jnp.int32) * local_rows
    else:
        left_wide = lax.all_gather(project(flat, left_weight), plane, axis=1, tiled=True)
        mask_wide = lax.all_gather(narrow_mask, plane, axis=1, tiled=True)
        turn = lambda a: lax.all_to_all(a, "row", split_axis=1, concat_axis=0, tiled=True)
        gather = lambda a: lax.all_gather(a, "row", axis=0, tiled=True)
        row_side = [beside(turn(left_wide), turn(mask_wide))]
        col_side = [beside(gather(project(flat, right_weight)), gather(narrow_mask))]
        places = jnp.zeros((2,), jnp.int32)

    split = output_weight.reshape(width // turns, turns, width, channels)
    weight = jnp.stack(
        [jnp.roll(split, u, axis=1).reshape(width * width, channels) for u in range(turns)]
    )
    gate_up = jnp.concatenate([gate_weight * 0.5, up_weight], axis=1).astype(jnp.bfloat16)
    conv_weight = kernel_weight.transpose(1, 2, 0, 3).reshape(3 * channels, 3 * channels)
    base = jnp.swapaxes(pair_input, 0, 1)

    sides = arrange(places, row_side, col_side, width, rows_dev, cols_dev)

    def run(first, strip, after=None):
        row_channels = sides[0]
        if after is not None:
            row_channels, _ = lax.optimization_barrier((row_channels, after))
        return tile_strip(
            first, strip, row_channels, *sides[1:], base, weight, gate_up, down_weight
        )

    ahead = lambda size: [(n, n + 1) for n in range(size - 1)]
    back = lambda size: [(n + 1, n) for n in range(size - 1)]

    if square and cols_dev % (8 * unit) == 0 and x_count > 1:
        part = cols_dev // 8
        host = lambda r, c: place_of(r, (r // core_count) * core_count + c % core_count)
        away = [(r, c) for r, c in tiles if r // core_count != c // core_count]
        near = [(r, c) for r, c in tiles if r // core_count == c // core_count]
        to_host = [(place_of(r, c), host(r, c)) for r, c in away]
        from_host = [(host(r, c), place_of(c, r)) for r, c in away]
        beside_pairs = [(place_of(r, c), place_of(c, r)) for r, c in near]
        send = lambda value, pairs: lax.ppermute(value, whole, pairs)
        opening = run(0, 3 * part)
        hosted = send(opening, to_host)
        mirrored_near = send(opening, beside_pairs)
        rest = run(3 * part, 5 * part, opening)
        mirrored_rest = send(rest, mirror_pairs)
        mirrored_away = send(hosted, from_host)
        turned = jnp.concatenate([opening, rest], axis=0)
        mirrored = [[mirrored_away, mirrored_near], [mirrored_rest]]
    else:
        turned = run(0, cols_dev)
        share = rows_dev // col_count
        fold = row_count // col_count
        second = lax.all_to_all(
            lax.all_to_all(
                jnp.swapaxes(turned, 0, 1), plane, split_axis=0, concat_axis=1, tiled=True
            ),
            "row",
            split_axis=1,
            concat_axis=0,
            tiled=True,
        )
        third = lax.all_to_all(
            jnp.swapaxes(second, 0, 1), plane, split_axis=1, concat_axis=1, tiled=True
        )
        full = (
            third.reshape(rows_dev, col_count, fold, share, channels)
            .transpose(0, 2, 1, 3, 4)
            .reshape(rows_dev, cols_dev, channels)
        )
        mirrored = [[full]]

    pair_two = jnp.swapaxes(turned, 0, 1)
    valid_i = lax.dynamic_slice_in_dim(token_valid, row_index * rows_dev, rows_dev)
    valid_j = lax.dynamic_slice_in_dim(token_valid, col_index * cols_dev, cols_dev)
    keep_i = valid_i.astype(jnp.float32)[:, None]
    keep_j = valid_j.astype(jnp.float32)[:, None]
    last_i, last_j = rows_dev - 1, cols_dev - 1
    parts = [[a.astype(jnp.float32) for a in part] for part in mirrored]
    along = lambda pick: jnp.concatenate([sum(pick(a) for a in part) for part in parts], axis=0)

    def edge(own, other, keep):
        return ((own.astype(jnp.float32) + other) * 0.5 * keep).astype(jnp.bfloat16)

    first_line = edge(turned[:, 0], sum(a[0] for a in parts[0]), keep_j * keep_i[0])
    last_line = edge(turned[:, -1], sum(a[-1] for a in parts[-1]), keep_j * keep_i[last_i])
    first_side = edge(turned[0], along(lambda a: a[:, 0]), keep_i * keep_j[0])
    last_side = edge(turned[-1], along(lambda a: a[:, -1]), keep_i * keep_j[last_j])
    left = lax.ppermute(last_side, plane, ahead(col_count))
    right = lax.ppermute(first_side, plane, back(col_count))
    border = lambda i, line: jnp.concatenate([left[i][None], line, right[i][None]], axis=0)
    top = lax.ppermute(border(last_i, last_line), "row", ahead(row_count))
    bottom = lax.ppermute(border(0, first_line), "row", back(row_count))
    left = jnp.concatenate([top[:1], left, bottom[:1]], axis=0)
    right = jnp.concatenate([top[-1:], right, bottom[-1:]], axis=0)
    wide_valid = jnp.broadcast_to(keep_j, (cols_dev, channels))
    return convolve(
        pair_two,
        mirrored,
        valid_i,
        wide_valid,
        [top[1:-1], bottom[1:-1], left, right],
        conv_weight,
    )


def solution(mesh):
    placed = (
        P(("groups", "row"), plane, None),
        P("row", ("groups", "col", "chan"), None),
        P("row", ("groups", "col", "chan")),
        P("groups"),
        P(),
        P(),
        P(),
        P(),
        P(),
        P(),
        P(),
    )
    return jax.shard_map(
        on_device,
        mesh=mesh,
        in_specs=placed,
        out_specs=P(("groups", "row"), plane, None),
        check_vma=False,
    )
```

```python
import functools
import math

import jax
import jax.numpy as jnp
from jax import lax
from jax.experimental import pallas as pl
from jax.experimental.pallas import tpu as pltpu
from jax.sharding import PartitionSpec as P

epsilon = 1e-05
lanes = 128
turns = 4
plane = ("col", "chan")
whole = ("row", "col", "chan")
unit = 8


def kernel_params(mib):
    return pltpu.CompilerParams(vmem_limit_bytes=mib * 1024 * 1024)


def project_kernel(features, mask, left_weight, right_weight, left, right):
    depth, tokens = mask.shape
    width, inner = left_weight.shape
    group = lanes // width

    def chosen(rows, columns, test):
        a = lax.broadcasted_iota(jnp.int32, (rows, columns), 0)
        b = lax.broadcasted_iota(jnp.int32, (rows, columns), 1)
        return jnp.where(test(a, b), 1.0, 0.0).astype(jnp.bfloat16)

    dot = lambda a, b: jnp.dot(a, b, preferred_element_type=jnp.float32)
    repeat_rows = chosen(group * inner, inner, lambda a, b: a % inner == b)
    repeat_lanes = chosen(width, lanes, lambda a, b: a == b % width)
    own_block = chosen(group * inner, lanes, lambda a, b: a // inner == b // width)
    spread = []
    for weight in (left_weight, right_weight):
        tall = lax.dot_general(
            repeat_rows,
            weight[...],
            (((1,), (1,)), ((), ())),
            preferred_element_type=jnp.float32,
        ).astype(jnp.bfloat16)
        spread.append(dot(tall, repeat_lanes).astype(jnp.bfloat16) * own_block)
    both = jnp.concatenate(spread, axis=1)
    kept = mask[...].astype(jnp.float32).astype(jnp.bfloat16)
    wide_mask = dot(kept, chosen(tokens, tokens * width, lambda a, b: a == b // width))
    for g in range(tokens // group):
        at = slice(g * lanes, (g + 1) * lanes)
        value = dot(features[:, g * group * inner : (g + 1) * group * inner], both)
        left[:, at] = (value[:, :lanes] * wide_mask[:, at]).astype(jnp.bfloat16)
        right[:, at] = (value[:, lanes:] * wide_mask[:, at]).astype(jnp.bfloat16)
    narrow = dot(kept, chosen(tokens, lanes, lambda a, b: a == b)).astype(jnp.bfloat16)
    left[:, tokens * width :] = narrow
    right[:, tokens * width :] = narrow


def project_sides(features, mask, left_weight, right_weight):
    depth, tokens = mask.shape
    span = tokens * left_weight.shape[1] + lanes
    in_vmem = pl.BlockSpec(memory_space=pltpu.VMEM)
    return pl.pallas_call(
        project_kernel,
        in_specs=[in_vmem] * 4,
        out_specs=[in_vmem] * 2,
        out_shape=[jax.ShapeDtypeStruct((depth, span), jnp.bfloat16)] * 2,
        compiler_params=kernel_params(8),
        cost_estimate=pl.CostEstimate(flops=1024, bytes_accessed=1024, transcendentals=0),
    )(features.reshape(depth, -1), mask, left_weight.T, right_weight.T)


def arrange_kernel(
    places, *refs, row_blocks, col_blocks, width, tokens_row, tokens_col
):
    row_refs, refs = refs[:row_blocks], refs[row_blocks:]
    col_refs, refs = refs[:col_blocks], refs[col_blocks:]
    row_side, lane_side, scale, gathered, turned, row_mask, col_mask = refs
    high = width // turns
    row_span, col_span = tokens_row * width, tokens_col * width
    for n, block in enumerate(row_refs):
        at = pl.ds(pl.multiple_of(places[n], 16), block.shape[0])
        gathered[at, :] = block[:, :row_span]
        row_mask[at, :] = block[:, row_span:]
    for n, block in enumerate(col_refs):
        at = pl.ds(pl.multiple_of(places[row_blocks + n], 16), block.shape[0])
        col_mask[at, :] = block[:, col_span:]
        for g in range(col_span // lanes):
            spot = slice(g * lanes, (g + 1) * lanes)
            piece = block[:, spot]
            lane_side[0, at, spot] = piece
            piece = piece.astype(jnp.float32)
            for turn in range(1, turns):
                lane_side[turn, at, spot] = pltpu.roll(piece, turn * width, 1).astype(jnp.bfloat16)
    for n in range(row_span // lanes):
        spot = slice(n * lanes, (n + 1) * lanes)
        turned[spot, :] = gathered[:, spot].astype(jnp.float32).T
    for channel in range(width):
        spot = ((channel % turns) * high + channel // turns) * tokens_row
        rows = turned[pl.ds(channel, tokens_row, stride=width), :]
        row_side[spot : spot + tokens_row, :] = rows.astype(jnp.bfloat16)
    counts = lax.dot_general(
        row_mask[...],
        col_mask[...],
        (((0,), (0,)), ((), ())),
        preferred_element_type=jnp.float32,
    )[:tokens_row]
    inverse = 1.0 / jnp.maximum(counts, 1.0)
    strip = scale.shape[0]
    for n in range(strip):
        count = tokens_col // strip
        scale[n, :, :count] = inverse[:, n * count : (n + 1) * count]


def arrange(places, row_side, col_side, width, tokens_row, tokens_col):
    depth = sum(block.shape[0] for block in row_side)
    body = functools.partial(
        arrange_kernel,
        row_blocks=len(row_side),
        col_blocks=len(col_side),
        width=width,
        tokens_row=tokens_row,
        tokens_col=tokens_col,
    )
    in_vmem = pl.BlockSpec(memory_space=pltpu.VMEM)
    return pl.pallas_call(
        body,
        in_specs=[pl.BlockSpec(memory_space=pltpu.SMEM)]
        + [in_vmem] * (len(row_side) + len(col_side)),
        out_specs=[in_vmem] * 3,
        out_shape=[
            jax.ShapeDtypeStruct((tokens_row * width, depth), jnp.bfloat16),
            jax.ShapeDtypeStruct((turns, depth, tokens_col * width), jnp.bfloat16),
            jax.ShapeDtypeStruct((tokens_col // unit, tokens_row, lanes), jnp.float32),
        ],
        scratch_shapes=[
            pltpu.VMEM((depth, tokens_row * width), jnp.bfloat16),
            pltpu.VMEM((tokens_row * width, depth), jnp.float32),
            pltpu.VMEM((depth, lanes), jnp.bfloat16),
            pltpu.VMEM((depth, lanes), jnp.bfloat16),
        ],
        compiler_params=kernel_params(12),
        cost_estimate=pl.CostEstimate(flops=1024, bytes_accessed=1024, transcendentals=0),
    )(places, *row_side, *col_side)


def transition_rows(values, gate_up, down):
    channels = values.shape[1]
    mean_of = jnp.full((channels, channels), 1.0 / channels, jnp.bfloat16)
    centre = jnp.dot(values.astype(jnp.bfloat16), mean_of, preferred_element_type=jnp.float32)
    offset = values - centre
    squares = (offset * offset).astype(jnp.bfloat16)
    spread = jnp.dot(squares, mean_of, preferred_element_type=jnp.float32)
    normed = (offset * lax.rsqrt(spread + epsilon)).astype(jnp.bfloat16)
    both = jnp.dot(normed, gate_up, preferred_element_type=jnp.float32)
    hidden_width = gate_up.shape[1] // 2
    half, up = both[:, :hidden_width], both[:, hidden_width:]
    hidden = ((half + half * jnp.tanh(half)) * up).astype(jnp.bfloat16)
    return values + jnp.dot(hidden, down, preferred_element_type=jnp.float32)


def tile_kernel(
    row_side,
    lane_side,
    scale,
    base,
    weight,
    gate_up,
    down,
    out,
    products,
    stacked,
    held,
    *,
    first,
    width,
):
    strip, tokens_row, channels = out.shape
    high = width // turns
    groups = strip // turns
    span = high * tokens_row
    for turn in range(turns):
        products[turn] = jnp.dot(
            row_side[turn * span : (turn + 1) * span, :],
            lane_side[turn, :, first * width : (first + strip) * width],
            preferred_element_type=jnp.float32,
        ).astype(jnp.bfloat16)
    position = lax.broadcasted_iota(jnp.int32, (tokens_row, lanes), 1) // width
    for g in range(groups):
        for h in range(high):
            parts = [
                products[t, h * tokens_row : (h + 1) * tokens_row, g * lanes : (g + 1) * lanes]
                for t in range(turns)
            ]
            for u in range(turns):
                mixed = parts[(turns - 1 - u) % turns]
                for t in range(turns - 1):
                    mixed = jnp.where(position == t, parts[(t - u) % turns], mixed)
                stacked[
                    u, g * tokens_row : (g + 1) * tokens_row, h * lanes : (h + 1) * lanes
                ] = mixed
    for u in range(turns):
        update = jnp.dot(stacked[u], weight[u], preferred_element_type=jnp.float32)
        for g in range(groups):
            n = turns * g + u
            at = first + n
            factor = scale[at // unit][:, at % unit : at % unit + 1]
            value = update[g * tokens_row : (g + 1) * tokens_row] * factor
            value = base[at].astype(jnp.float32) + value
            held[n * tokens_row : (n + 1) * tokens_row, :] = value.astype(jnp.bfloat16)
    piece = strip if strip <= 32 else strip // 2
    for start in range(0, strip, piece):
        at = slice(start * tokens_row, (start + piece) * tokens_row)
        result = transition_rows(held[at, :].astype(jnp.float32), gate_up[...], down[...])
        out[start : start + piece] = result.astype(out.dtype).reshape(piece, tokens_row, channels)


def tile_strip(first, strip, row_side, lane_side, scale, base, weight, gate_up, down):
    tokens_row, channels = base.shape[1:]
    width = lane_side.shape[2] // base.shape[0]
    operands = [row_side, lane_side, scale, base, weight, gate_up, down]
    in_vmem = pl.BlockSpec(memory_space=pltpu.VMEM)
    return pl.pallas_call(
        functools.partial(tile_kernel, first=first, width=width),
        in_specs=[in_vmem] * len(operands),
        out_specs=in_vmem,
        out_shape=jax.ShapeDtypeStruct((strip, tokens_row, channels), jnp.bfloat16),
        scratch_shapes=[
            pltpu.VMEM((turns, tokens_row * width // turns, strip * width), jnp.bfloat16),
            pltpu.VMEM((turns, strip // turns * tokens_row, width * width), jnp.bfloat16),
            pltpu.VMEM((strip * tokens_row, channels), jnp.bfloat16),
        ],
        compiler_params=kernel_params(40),
        cost_estimate=pl.CostEstimate(flops=1024, bytes_accessed=1024, transcendentals=0),
    )(*operands)


def conv_kernel(
    valid_i, pair_two, *refs, parts
):
    counts = [len(p) for p in parts]
    total_parts = sum(counts)
    mirrored, refs = refs[:total_parts], refs[total_parts:]
    valid_j, top, bottom, left, right, weight, out, padded, centre = refs
    step = pl.program_id(0)
    rows, columns, channels = pair_two.shape
    strip = out.shape[0]

    @pl.when(step == 0)
    def _():
        padded[0, 8 : 8 + columns, :] = top[...].astype(jnp.float32)
        padded[rows + 1, 8 : 8 + columns, :] = bottom[...].astype(jnp.float32)
        i = 0
        used = 0
        for count in counts:
            group = mirrored[used : used + count]
            used += count
            for n in range(group[0].shape[0]):
                other = group[0][n].astype(jnp.float32)
                for more in group[1:]:
                    other = other + more[n].astype(jnp.float32)
                symmetric = (pair_two[i].astype(jnp.float32) + other) * 0.5
                centre[i] = symmetric
                keep = valid_j[...] * valid_i[i].astype(jnp.float32)
                padded[i + 1, 8 : 8 + columns, :] = symmetric * keep
                i += 1
        for i in range(rows + 2):
            padded[i, 7:8, :] = left[i : i + 1, :].astype(jnp.float32)
            padded[i, 8 + columns : 9 + columns, :] = right[i : i + 1, :].astype(jnp.float32)

    window = padded.at[pl.ds(step * strip, strip + 2)]
    shifted = [
        window[:, 7 + b : 7 + b + columns, :]
        .astype(jnp.bfloat16)
        .reshape((strip + 2) * columns, channels)
        for b in range(3)
    ]
    taps = jnp.dot(
        jnp.concatenate(shifted, axis=1), weight[...], preferred_element_type=jnp.float32
    ).reshape(strip + 2, columns, 3 * channels)
    total = centre[pl.ds(step * strip, strip)]
    for a in range(3):
        total = total + taps[a : a + strip, :, a * channels : (a + 1) * channels]
    out[...] = total.astype(out.dtype)


def convolve(pair_two, mirrored, valid_i, valid_j, halos, weight):
    rows, columns, channels = pair_two.shape
    strip = math.gcd(32, rows)
    operands = [pair_two, *[a for part in mirrored for a in part], valid_j, *halos, weight]
    fixed = lambda a: pl.BlockSpec(a.shape, lambda n, rank=a.ndim: (0,) * rank)
    return pl.pallas_call(
        functools.partial(conv_kernel, parts=[tuple(range(len(part))) for part in mirrored]),
        grid=(rows // strip,),
        in_specs=[pl.BlockSpec(memory_space=pltpu.SMEM)] + [fixed(a) for a in operands],
        out_specs=pl.BlockSpec((strip, columns, channels), lambda n: (n, 0, 0)),
        out_shape=jax.ShapeDtypeStruct(pair_two.shape, jnp.bfloat16),
        scratch_shapes=[
            pltpu.VMEM((rows + 2, columns + 16, channels), jnp.float32),
            pltpu.VMEM((rows, columns, channels), jnp.float32),
        ],
        compiler_params=kernel_params(40),
        cost_estimate=pl.CostEstimate(
            flops=18 * rows * columns * channels * channels,
            bytes_accessed=3 << 20,
            transcendentals=0,
        ),
    )(valid_i, *operands)


def shifts(size, step):
    return [(n, (n + step) % size) for n in range(size)]


def on_device(
    pair_input,
    alignment_features,
    alignment_mask,
    token_valid,
    left_weight,
    right_weight,
    output_weight,
    gate_weight,
    up_weight,
    down_weight,
    kernel_weight,
):
    rows_dev, cols_dev, channels = pair_input.shape
    local_rows, local_tokens, align_width = alignment_features.shape
    width = left_weight.shape[1]
    row_count, col_count = lax.axis_size("row"), lax.axis_size(plane)
    x_count, core_count = lax.axis_size("col"), lax.axis_size("chan")
    row_index, col_index = lax.axis_index("row"), lax.axis_index(plane)
    x_index, core_index = lax.axis_index("col"), lax.axis_index("chan")
    square = row_count == col_count
    tiles = [(r, c) for r in range(row_count) for c in range(col_count)]
    place_of = lambda r, c: r * col_count + c

    flat = alignment_features.reshape(local_rows * local_tokens, align_width)
    mask_rows = alignment_mask.astype(jnp.float32)

    def project(flat, weight):
        value = jnp.dot(flat, weight, preferred_element_type=jnp.float32)
        value = value.reshape(local_rows, local_tokens, width) * mask_rows[:, :, None]
        return value.astype(jnp.bfloat16)

    narrow_mask = alignment_mask.astype(jnp.bfloat16)

    def beside(side, mask):
        depth, tokens = mask.shape
        room = jnp.pad(mask, ((0, 0), (0, lanes - tokens % lanes)))
        return jnp.concatenate([side.reshape(depth, tokens * width), room], axis=1)

    if square:
        left_block, right_block = project_sides(
            alignment_features, alignment_mask, left_weight, right_weight
        )
        mirror_pairs = [(place_of(r, c), place_of(c, r)) for r, c in tiles]
        first = lax.ppermute(left_block, whole, mirror_pairs)
        col_side, col_places = [right_block], [row_index]
        held_back, _ = lax.optimization_barrier((right_block, first))
        for step in range(1, row_count):
            block = right_block if step in (1, row_count - 1) else held_back
            col_side.append(lax.ppermute(block, "row", shifts(row_count, -step)))
            col_places.append((row_index + step) % row_count)
        row_side, row_places = [first], [col_index]
        for step in range(1, x_count):
            row_side.append(lax.ppermute(first, "col", shifts(x_count, -step)))
            row_places.append(((x_index + step) % x_count) * core_count + core_index)
        for step in range(1, core_count):
            for n in range(x_count):
                row_side.append(lax.ppermute(row_side[n], "chan", shifts(core_count, -step)))
                row_places.append(
                    ((x_index + n) % x_count) * core_count + (core_index + step) % core_count
                )
        places = jnp.stack(row_places + col_places).astype(jnp.int32) * local_rows
    else:
        left_wide = lax.all_gather(project(flat, left_weight), plane, axis=1, tiled=True)
        mask_wide = lax.all_gather(narrow_mask, plane, axis=1, tiled=True)
        turn = lambda a: lax.all_to_all(a, "row", split_axis=1, concat_axis=0, tiled=True)
        gather = lambda a: lax.all_gather(a, "row", axis=0, tiled=True)
        row_side = [beside(turn(left_wide), turn(mask_wide))]
        col_side = [beside(gather(project(flat, right_weight)), gather(narrow_mask))]
        places = jnp.zeros((2,), jnp.int32)

    split = output_weight.reshape(width // turns, turns, width, channels)
    weight = jnp.stack(
        [jnp.roll(split, u, axis=1).reshape(width * width, channels) for u in range(turns)]
    )
    gate_up = jnp.concatenate([gate_weight * 0.5, up_weight], axis=1).astype(jnp.bfloat16)
    conv_weight = kernel_weight.transpose(1, 2, 0, 3).reshape(3 * channels, 3 * channels)
    base = jnp.swapaxes(pair_input, 0, 1)

    sides = arrange(places, row_side, col_side, width, rows_dev, cols_dev)

    def run(first, strip, after=None):
        row_channels = sides[0]
        if after is not None:
            row_channels, _ = lax.optimization_barrier((row_channels, after))
        return tile_strip(
            first, strip, row_channels, *sides[1:], base, weight, gate_up, down_weight
        )

    ahead = lambda size: [(n, n + 1) for n in range(size - 1)]
    back = lambda size: [(n + 1, n) for n in range(size - 1)]

    if square and cols_dev % (8 * unit) == 0 and x_count > 1:
        part = cols_dev // 8
        host = lambda r, c: place_of(r, (r // core_count) * core_count + c % core_count)
        away = [(r, c) for r, c in tiles if r // core_count != c // core_count]
        near = [(r, c) for r, c in tiles if r // core_count == c // core_count]
        to_host = [(place_of(r, c), host(r, c)) for r, c in away]
        from_host = [(host(r, c), place_of(c, r)) for r, c in away]
        beside_pairs = [(place_of(r, c), place_of(c, r)) for r, c in near]
        send = lambda value, pairs: lax.ppermute(value, whole, pairs)
        opening = run(0, 3 * part)
        hosted = send(opening, to_host)
        mirrored_near = send(opening, beside_pairs)
        rest = run(3 * part, 5 * part, opening)
        mirrored_rest = send(rest, mirror_pairs)
        mirrored_away = send(hosted, from_host)
        turned = jnp.concatenate([opening, rest], axis=0)
        mirrored = [[mirrored_away, mirrored_near], [mirrored_rest]]
    else:
        turned = run(0, cols_dev)
        share = rows_dev // col_count
        fold = row_count // col_count
        second = lax.all_to_all(
            lax.all_to_all(
                jnp.swapaxes(turned, 0, 1), plane, split_axis=0, concat_axis=1, tiled=True
            ),
            "row",
            split_axis=1,
            concat_axis=0,
            tiled=True,
        )
        third = lax.all_to_all(
            jnp.swapaxes(second, 0, 1), plane, split_axis=1, concat_axis=1, tiled=True
        )
        full = (
            third.reshape(rows_dev, col_count, fold, share, channels)
            .transpose(0, 2, 1, 3, 4)
            .reshape(rows_dev, cols_dev, channels)
        )
        mirrored = [[full]]

    pair_two = jnp.swapaxes(turned, 0, 1)
    valid_i = lax.dynamic_slice_in_dim(token_valid, row_index * rows_dev, rows_dev)
    valid_j = lax.dynamic_slice_in_dim(token_valid, col_index * cols_dev, cols_dev)
    keep_i = valid_i.astype(jnp.float32)[:, None]
    keep_j = valid_j.astype(jnp.float32)[:, None]
    last_i, last_j = rows_dev - 1, cols_dev - 1
    parts = [[a.astype(jnp.float32) for a in part] for part in mirrored]
    along = lambda pick: jnp.concatenate([sum(pick(a) for a in part) for part in parts], axis=0)

    def edge(own, other, keep):
        return ((own.astype(jnp.float32) + other) * 0.5 * keep).astype(jnp.bfloat16)

    first_line = edge(turned[:, 0], sum(a[0] for a in parts[0]), keep_j * keep_i[0])
    last_line = edge(turned[:, -1], sum(a[-1] for a in parts[-1]), keep_j * keep_i[last_i])
    first_side = edge(turned[0], along(lambda a: a[:, 0]), keep_i * keep_j[0])
    last_side = edge(turned[-1], along(lambda a: a[:, -1]), keep_i * keep_j[last_j])
    left = lax.ppermute(last_side, plane, ahead(col_count))
    right = lax.ppermute(first_side, plane, back(col_count))
    border = lambda i, line: jnp.concatenate([left[i][None], line, right[i][None]], axis=0)
    top = lax.ppermute(border(last_i, last_line), "row", ahead(row_count))
    bottom = lax.ppermute(border(0, first_line), "row", back(row_count))
    left = jnp.concatenate([top[:1], left, bottom[:1]], axis=0)
    right = jnp.concatenate([top[-1:], right, bottom[-1:]], axis=0)
    wide_valid = jnp.broadcast_to(keep_j, (cols_dev, channels))
    return convolve(
        pair_two,
        mirrored,
        valid_i,
        wide_valid,
        [top[1:-1], bottom[1:-1], left, right],
        conv_weight,
    )


def solution(mesh):
    placed = (
        P(("groups", "row"), plane, None),
        P("row", ("groups", "col", "chan"), None),
        P("row", ("groups", "col", "chan")),
        P("groups"),
        P(),
        P(),
        P(),
        P(),
        P(),
        P(),
        P(),
    )
    return jax.shard_map(
        on_device,
        mesh=mesh,
        in_specs=placed,
        out_specs=P(("groups", "row"), plane, None),
        check_vma=False,
    )
```

```python
import functools
import math

import jax
import jax.numpy as jnp
from jax import lax
from jax.experimental import pallas as pl
from jax.experimental.pallas import tpu as pltpu
from jax.sharding import PartitionSpec as P

epsilon = 1e-05
lanes = 128
turns = 4
plane = ("col", "chan")
whole = ("row", "col", "chan")
unit = 8


def kernel_params(mib):
    return pltpu.CompilerParams(vmem_limit_bytes=mib * 1024 * 1024)


def project_kernel(features, mask, left_weight, right_weight, left, right):
    depth, tokens = mask.shape
    width, inner = left_weight.shape
    group = lanes // width

    def chosen(rows, columns, test):
        a = lax.broadcasted_iota(jnp.int32, (rows, columns), 0)
        b = lax.broadcasted_iota(jnp.int32, (rows, columns), 1)
        return jnp.where(test(a, b), 1.0, 0.0).astype(jnp.bfloat16)

    dot = lambda a, b: jnp.dot(a, b, preferred_element_type=jnp.float32)
    repeat_rows = chosen(group * inner, inner, lambda a, b: a % inner == b)
    repeat_lanes = chosen(width, lanes, lambda a, b: a == b % width)
    own_block = chosen(group * inner, lanes, lambda a, b: a // inner == b // width)
    spread = []
    for weight in (left_weight, right_weight):
        tall = lax.dot_general(
            repeat_rows,
            weight[...],
            (((1,), (1,)), ((), ())),
            preferred_element_type=jnp.float32,
        ).astype(jnp.bfloat16)
        spread.append(dot(tall, repeat_lanes).astype(jnp.bfloat16) * own_block)
    both = jnp.concatenate(spread, axis=1)
    kept = mask[...].astype(jnp.float32).astype(jnp.bfloat16)
    wide_mask = dot(kept, chosen(tokens, tokens * width, lambda a, b: a == b // width))
    for g in range(tokens // group):
        at = slice(g * lanes, (g + 1) * lanes)
        value = dot(features[:, g * group * inner : (g + 1) * group * inner], both)
        left[:, at] = (value[:, :lanes] * wide_mask[:, at]).astype(jnp.bfloat16)
        right[:, at] = (value[:, lanes:] * wide_mask[:, at]).astype(jnp.bfloat16)
    narrow = dot(kept, chosen(tokens, lanes, lambda a, b: a == b)).astype(jnp.bfloat16)
    left[:, tokens * width :] = narrow
    right[:, tokens * width :] = narrow


def project_sides(features, mask, left_weight, right_weight):
    depth, tokens = mask.shape
    span = tokens * left_weight.shape[1] + lanes
    in_vmem = pl.BlockSpec(memory_space=pltpu.VMEM)
    return pl.pallas_call(
        project_kernel,
        in_specs=[in_vmem] * 4,
        out_specs=[in_vmem] * 2,
        out_shape=[jax.ShapeDtypeStruct((depth, span), jnp.bfloat16)] * 2,
        compiler_params=kernel_params(8),
        cost_estimate=pl.CostEstimate(flops=1024, bytes_accessed=1024, transcendentals=0),
    )(features.reshape(depth, -1), mask, left_weight.T, right_weight.T)


def arrange_kernel(
    places, *refs, row_blocks, col_blocks, width, tokens_row, tokens_col
):
    row_refs, refs = refs[:row_blocks], refs[row_blocks:]
    col_refs, refs = refs[:col_blocks], refs[col_blocks:]
    row_side, lane_side, scale, gathered, turned, row_mask, col_mask = refs
    high = width // turns
    row_span, col_span = tokens_row * width, tokens_col * width
    for n, block in enumerate(row_refs):
        at = pl.ds(pl.multiple_of(places[n], 16), block.shape[0])
        gathered[at, :] = block[:, :row_span]
        row_mask[at, :] = block[:, row_span:]
    for n, block in enumerate(col_refs):
        at = pl.ds(pl.multiple_of(places[row_blocks + n], 16), block.shape[0])
        col_mask[at, :] = block[:, col_span:]
        for g in range(col_span // lanes):
            spot = slice(g * lanes, (g + 1) * lanes)
            piece = block[:, spot]
            lane_side[0, at, spot] = piece
            piece = piece.astype(jnp.float32)
            for turn in range(1, turns):
                lane_side[turn, at, spot] = pltpu.roll(piece, turn * width, 1).astype(jnp.bfloat16)
    for n in range(row_span // lanes):
        spot = slice(n * lanes, (n + 1) * lanes)
        turned[spot, :] = gathered[:, spot].astype(jnp.float32).T
    for channel in range(width):
        spot = ((channel % turns) * high + channel // turns) * tokens_row
        rows = turned[pl.ds(channel, tokens_row, stride=width), :]
        row_side[spot : spot + tokens_row, :] = rows.astype(jnp.bfloat16)
    counts = lax.dot_general(
        row_mask[...],
        col_mask[...],
        (((0,), (0,)), ((), ())),
        preferred_element_type=jnp.float32,
    )[:tokens_row]
    inverse = 1.0 / jnp.maximum(counts, 1.0)
    strip = scale.shape[0]
    for n in range(strip):
        count = tokens_col // strip
        scale[n, :, :count] = inverse[:, n * count : (n + 1) * count]


def arrange(places, row_side, col_side, width, tokens_row, tokens_col):
    depth = sum(block.shape[0] for block in row_side)
    body = functools.partial(
        arrange_kernel,
        row_blocks=len(row_side),
        col_blocks=len(col_side),
        width=width,
        tokens_row=tokens_row,
        tokens_col=tokens_col,
    )
    in_vmem = pl.BlockSpec(memory_space=pltpu.VMEM)
    return pl.pallas_call(
        body,
        in_specs=[pl.BlockSpec(memory_space=pltpu.SMEM)]
        + [in_vmem] * (len(row_side) + len(col_side)),
        out_specs=[in_vmem] * 3,
        out_shape=[
            jax.ShapeDtypeStruct((tokens_row * width, depth), jnp.bfloat16),
            jax.ShapeDtypeStruct((turns, depth, tokens_col * width), jnp.bfloat16),
            jax.ShapeDtypeStruct((tokens_col // unit, tokens_row, lanes), jnp.float32),
        ],
        scratch_shapes=[
            pltpu.VMEM((depth, tokens_row * width), jnp.bfloat16),
            pltpu.VMEM((tokens_row * width, depth), jnp.float32),
            pltpu.VMEM((depth, lanes), jnp.bfloat16),
            pltpu.VMEM((depth, lanes), jnp.bfloat16),
        ],
        compiler_params=kernel_params(12),
        cost_estimate=pl.CostEstimate(flops=1024, bytes_accessed=1024, transcendentals=0),
    )(places, *row_side, *col_side)


def transition_rows(values, gate_up, down):
    channels = values.shape[1]
    mean_of = jnp.full((channels, channels), 1.0 / channels, jnp.bfloat16)
    centre = jnp.dot(values.astype(jnp.bfloat16), mean_of, preferred_element_type=jnp.float32)
    offset = values - centre
    squares = (offset * offset).astype(jnp.bfloat16)
    spread = jnp.dot(squares, mean_of, preferred_element_type=jnp.float32)
    normed = (offset * lax.rsqrt(spread + epsilon)).astype(jnp.bfloat16)
    both = jnp.dot(normed, gate_up, preferred_element_type=jnp.float32)
    hidden_width = gate_up.shape[1] // 2
    half, up = both[:, :hidden_width], both[:, hidden_width:]
    hidden = ((half + half * jnp.tanh(half)) * up).astype(jnp.bfloat16)
    return values + jnp.dot(hidden, down, preferred_element_type=jnp.float32)


def tile_kernel(
    row_side,
    lane_side,
    scale,
    base,
    weight,
    gate_up,
    down,
    out,
    products,
    stacked,
    held,
    *,
    first,
    width,
):
    strip, tokens_row, channels = out.shape
    high = width // turns
    groups = strip // turns
    span = high * tokens_row
    for turn in range(turns):
        products[turn] = jnp.dot(
            row_side[turn * span : (turn + 1) * span, :],
            lane_side[turn, :, first * width : (first + strip) * width],
            preferred_element_type=jnp.float32,
        ).astype(jnp.bfloat16)
    position = lax.broadcasted_iota(jnp.int32, (tokens_row, lanes), 1) // width
    for g in range(groups):
        for h in range(high):
            parts = [
                products[t, h * tokens_row : (h + 1) * tokens_row, g * lanes : (g + 1) * lanes]
                for t in range(turns)
            ]
            for u in range(turns):
                mixed = parts[(turns - 1 - u) % turns]
                for t in range(turns - 1):
                    mixed = jnp.where(position == t, parts[(t - u) % turns], mixed)
                stacked[
                    u, g * tokens_row : (g + 1) * tokens_row, h * lanes : (h + 1) * lanes
                ] = mixed
    for u in range(turns):
        update = jnp.dot(stacked[u], weight[u], preferred_element_type=jnp.float32)
        for g in range(groups):
            n = turns * g + u
            at = first + n
            factor = scale[at // unit][:, at % unit : at % unit + 1]
            value = update[g * tokens_row : (g + 1) * tokens_row] * factor
            value = base[at].astype(jnp.float32) + value
            held[n * tokens_row : (n + 1) * tokens_row, :] = value.astype(jnp.bfloat16)
    piece = strip if strip <= 32 else strip // 2
    for start in range(0, strip, piece):
        at = slice(start * tokens_row, (start + piece) * tokens_row)
        result = transition_rows(held[at, :].astype(jnp.float32), gate_up[...], down[...])
        out[start : start + piece] = result.astype(out.dtype).reshape(piece, tokens_row, channels)


def tile_strip(first, strip, row_side, lane_side, scale, base, weight, gate_up, down):
    tokens_row, channels = base.shape[1:]
    width = lane_side.shape[2] // base.shape[0]
    operands = [row_side, lane_side, scale, base, weight, gate_up, down]
    in_vmem = pl.BlockSpec(memory_space=pltpu.VMEM)
    return pl.pallas_call(
        functools.partial(tile_kernel, first=first, width=width),
        in_specs=[in_vmem] * len(operands),
        out_specs=in_vmem,
        out_shape=jax.ShapeDtypeStruct((strip, tokens_row, channels), jnp.bfloat16),
        scratch_shapes=[
            pltpu.VMEM((turns, tokens_row * width // turns, strip * width), jnp.bfloat16),
            pltpu.VMEM((turns, strip // turns * tokens_row, width * width), jnp.bfloat16),
            pltpu.VMEM((strip * tokens_row, channels), jnp.bfloat16),
        ],
        compiler_params=kernel_params(40),
        cost_estimate=pl.CostEstimate(flops=1024, bytes_accessed=1024, transcendentals=0),
    )(*operands)


def conv_kernel(
    valid_i, pair_two, *refs, parts
):
    counts = [len(p) for p in parts]
    total_parts = sum(counts)
    mirrored, refs = refs[:total_parts], refs[total_parts:]
    valid_j, top, bottom, left, right, weight, out, padded, centre = refs
    step = pl.program_id(0)
    rows, columns, channels = pair_two.shape
    strip = out.shape[0]

    @pl.when(step == 0)
    def _():
        padded[0, 8 : 8 + columns, :] = top[...].astype(jnp.float32)
        padded[rows + 1, 8 : 8 + columns, :] = bottom[...].astype(jnp.float32)
        i = 0
        used = 0
        for count in counts:
            group = mirrored[used : used + count]
            used += count
            for n in range(group[0].shape[0]):
                other = group[0][n].astype(jnp.float32)
                for more in group[1:]:
                    other = other + more[n].astype(jnp.float32)
                symmetric = (pair_two[i].astype(jnp.float32) + other) * 0.5
                centre[i] = symmetric
                keep = valid_j[...] * valid_i[i].astype(jnp.float32)
                padded[i + 1, 8 : 8 + columns, :] = symmetric * keep
                i += 1
        for i in range(rows + 2):
            padded[i, 7:8, :] = left[i : i + 1, :].astype(jnp.float32)
            padded[i, 8 + columns : 9 + columns, :] = right[i : i + 1, :].astype(jnp.float32)

    window = padded.at[pl.ds(step * strip, strip + 2)]
    shifted = [
        window[:, 7 + b : 7 + b + columns, :]
        .astype(jnp.bfloat16)
        .reshape((strip + 2) * columns, channels)
        for b in range(3)
    ]
    taps = jnp.dot(
        jnp.concatenate(shifted, axis=1), weight[...], preferred_element_type=jnp.float32
    ).reshape(strip + 2, columns, 3 * channels)
    total = centre[pl.ds(step * strip, strip)]
    for a in range(3):
        total = total + taps[a : a + strip, :, a * channels : (a + 1) * channels]
    out[...] = total.astype(out.dtype)


def convolve(pair_two, mirrored, valid_i, valid_j, halos, weight):
    rows, columns, channels = pair_two.shape
    strip = math.gcd(32, rows)
    operands = [pair_two, *[a for part in mirrored for a in part], valid_j, *halos, weight]
    fixed = lambda a: pl.BlockSpec(a.shape, lambda n, rank=a.ndim: (0,) * rank)
    return pl.pallas_call(
        functools.partial(conv_kernel, parts=[tuple(range(len(part))) for part in mirrored]),
        grid=(rows // strip,),
        in_specs=[pl.BlockSpec(memory_space=pltpu.SMEM)] + [fixed(a) for a in operands],
        out_specs=pl.BlockSpec((strip, columns, channels), lambda n: (n, 0, 0)),
        out_shape=jax.ShapeDtypeStruct(pair_two.shape, jnp.bfloat16),
        scratch_shapes=[
            pltpu.VMEM((rows + 2, columns + 16, channels), jnp.float32),
            pltpu.VMEM((rows, columns, channels), jnp.float32),
        ],
        compiler_params=kernel_params(40),
        cost_estimate=pl.CostEstimate(
            flops=18 * rows * columns * channels * channels,
            bytes_accessed=3 << 20,
            transcendentals=0,
        ),
    )(valid_i, *operands)


def shifts(size, step):
    return [(n, (n + step) % size) for n in range(size)]


def on_device(
    pair_input,
    alignment_features,
    alignment_mask,
    token_valid,
    left_weight,
    right_weight,
    output_weight,
    gate_weight,
    up_weight,
    down_weight,
    kernel_weight,
):
    rows_dev, cols_dev, channels = pair_input.shape
    local_rows, local_tokens, align_width = alignment_features.shape
    width = left_weight.shape[1]
    row_count, col_count = lax.axis_size("row"), lax.axis_size(plane)
    x_count, core_count = lax.axis_size("col"), lax.axis_size("chan")
    row_index, col_index = lax.axis_index("row"), lax.axis_index(plane)
    x_index, core_index = lax.axis_index("col"), lax.axis_index("chan")
    square = row_count == col_count
    tiles = [(r, c) for r in range(row_count) for c in range(col_count)]
    place_of = lambda r, c: r * col_count + c

    flat = alignment_features.reshape(local_rows * local_tokens, align_width)
    mask_rows = alignment_mask.astype(jnp.float32)

    def project(flat, weight):
        value = jnp.dot(flat, weight, preferred_element_type=jnp.float32)
        value = value.reshape(local_rows, local_tokens, width) * mask_rows[:, :, None]
        return value.astype(jnp.bfloat16)

    narrow_mask = alignment_mask.astype(jnp.bfloat16)

    def beside(side, mask):
        depth, tokens = mask.shape
        room = jnp.pad(mask, ((0, 0), (0, lanes - tokens % lanes)))
        return jnp.concatenate([side.reshape(depth, tokens * width), room], axis=1)

    if square:
        left_block, right_block = project_sides(
            alignment_features, alignment_mask, left_weight, right_weight
        )
        mirror_pairs = [(place_of(r, c), place_of(c, r)) for r, c in tiles]
        first = lax.ppermute(left_block, whole, mirror_pairs)
        col_side, col_places = [right_block], [row_index]
        held_back, _ = lax.optimization_barrier((right_block, first))
        for step in range(1, row_count):
            block = right_block if step in (1, row_count - 1) else held_back
            col_side.append(lax.ppermute(block, "row", shifts(row_count, -step)))
            col_places.append((row_index + step) % row_count)
        row_side, row_places = [first], [col_index]
        for step in range(1, x_count):
            row_side.append(lax.ppermute(first, "col", shifts(x_count, -step)))
            row_places.append(((x_index + step) % x_count) * core_count + core_index)
        for step in range(1, core_count):
            for n in range(x_count):
                row_side.append(lax.ppermute(row_side[n], "chan", shifts(core_count, -step)))
                row_places.append(
                    ((x_index + n) % x_count) * core_count + (core_index + step) % core_count
                )
        places = jnp.stack(row_places + col_places).astype(jnp.int32) * local_rows
    else:
        left_wide = lax.all_gather(project(flat, left_weight), plane, axis=1, tiled=True)
        mask_wide = lax.all_gather(narrow_mask, plane, axis=1, tiled=True)
        turn = lambda a: lax.all_to_all(a, "row", split_axis=1, concat_axis=0, tiled=True)
        gather = lambda a: lax.all_gather(a, "row", axis=0, tiled=True)
        row_side = [beside(turn(left_wide), turn(mask_wide))]
        col_side = [beside(gather(project(flat, right_weight)), gather(narrow_mask))]
        places = jnp.zeros((2,), jnp.int32)

    split = output_weight.reshape(width // turns, turns, width, channels)
    weight = jnp.stack(
        [jnp.roll(split, u, axis=1).reshape(width * width, channels) for u in range(turns)]
    )
    gate_up = jnp.concatenate([gate_weight * 0.5, up_weight], axis=1).astype(jnp.bfloat16)
    conv_weight = kernel_weight.transpose(1, 2, 0, 3).reshape(3 * channels, 3 * channels)
    base = jnp.swapaxes(pair_input, 0, 1)

    sides = arrange(places, row_side, col_side, width, rows_dev, cols_dev)

    def run(first, strip, after=None):
        row_channels = sides[0]
        if after is not None:
            row_channels, _ = lax.optimization_barrier((row_channels, after))
        return tile_strip(
            first, strip, row_channels, *sides[1:], base, weight, gate_up, down_weight
        )

    ahead = lambda size: [(n, n + 1) for n in range(size - 1)]
    back = lambda size: [(n + 1, n) for n in range(size - 1)]

    if square and cols_dev % (8 * unit) == 0 and x_count > 1:
        part = cols_dev // 16
        host = lambda r, c: place_of(r, (r // core_count) * core_count + c % core_count)
        away = [(r, c) for r, c in tiles if r // core_count != c // core_count]
        near = [(r, c) for r, c in tiles if r // core_count == c // core_count]
        to_host = [(place_of(r, c), host(r, c)) for r, c in away]
        from_host = [(host(r, c), place_of(c, r)) for r, c in away]
        beside_pairs = [(place_of(r, c), place_of(c, r)) for r, c in near]
        send = lambda value, pairs: lax.ppermute(value, whole, pairs)
        opening = run(0, 7 * part)
        hosted = send(opening, to_host)
        mirrored_near = send(opening, beside_pairs)
        middle = run(7 * part, 4 * part, opening)
        mirrored_middle = send(middle, mirror_pairs)
        mirrored_away = send(hosted, from_host)
        last = run(11 * part, 5 * part, (middle, hosted))
        mirrored_last = send(last, mirror_pairs)
        turned = jnp.concatenate([opening, middle, last], axis=0)
        mirrored = [[mirrored_away, mirrored_near], [mirrored_middle], [mirrored_last]]
    else:
        turned = run(0, cols_dev)
        share = rows_dev // col_count
        fold = row_count // col_count
        second = lax.all_to_all(
            lax.all_to_all(
                jnp.swapaxes(turned, 0, 1), plane, split_axis=0, concat_axis=1, tiled=True
            ),
            "row",
            split_axis=1,
            concat_axis=0,
            tiled=True,
        )
        third = lax.all_to_all(
            jnp.swapaxes(second, 0, 1), plane, split_axis=1, concat_axis=1, tiled=True
        )
        full = (
            third.reshape(rows_dev, col_count, fold, share, channels)
            .transpose(0, 2, 1, 3, 4)
            .reshape(rows_dev, cols_dev, channels)
        )
        mirrored = [[full]]

    pair_two = jnp.swapaxes(turned, 0, 1)
    valid_i = lax.dynamic_slice_in_dim(token_valid, row_index * rows_dev, rows_dev)
    valid_j = lax.dynamic_slice_in_dim(token_valid, col_index * cols_dev, cols_dev)
    keep_i = valid_i.astype(jnp.float32)[:, None]
    keep_j = valid_j.astype(jnp.float32)[:, None]
    last_i, last_j = rows_dev - 1, cols_dev - 1
    parts = [[a.astype(jnp.float32) for a in part] for part in mirrored]
    along = lambda pick: jnp.concatenate([sum(pick(a) for a in part) for part in parts], axis=0)

    def edge(own, other, keep):
        return ((own.astype(jnp.float32) + other) * 0.5 * keep).astype(jnp.bfloat16)

    first_line = edge(turned[:, 0], sum(a[0] for a in parts[0]), keep_j * keep_i[0])
    last_line = edge(turned[:, -1], sum(a[-1] for a in parts[-1]), keep_j * keep_i[last_i])
    first_side = edge(turned[0], along(lambda a: a[:, 0]), keep_i * keep_j[0])
    last_side = edge(turned[-1], along(lambda a: a[:, -1]), keep_i * keep_j[last_j])
    left = lax.ppermute(last_side, plane, ahead(col_count))
    right = lax.ppermute(first_side, plane, back(col_count))
    border = lambda i, line: jnp.concatenate([left[i][None], line, right[i][None]], axis=0)
    top = lax.ppermute(border(last_i, last_line), "row", ahead(row_count))
    bottom = lax.ppermute(border(0, first_line), "row", back(row_count))
    left = jnp.concatenate([top[:1], left, bottom[:1]], axis=0)
    right = jnp.concatenate([top[-1:], right, bottom[-1:]], axis=0)
    wide_valid = jnp.broadcast_to(keep_j, (cols_dev, channels))
    return convolve(
        pair_two,
        mirrored,
        valid_i,
        wide_valid,
        [top[1:-1], bottom[1:-1], left, right],
        conv_weight,
    )


def solution(mesh):
    placed = (
        P(("groups", "row"), plane, None),
        P("row", ("groups", "col", "chan"), None),
        P("row", ("groups", "col", "chan")),
        P("groups"),
        P(),
        P(),
        P(),
        P(),
        P(),
        P(),
        P(),
    )
    return jax.shard_map(
        on_device,
        mesh=mesh,
        in_specs=placed,
        out_specs=P(("groups", "row"), plane, None),
        check_vma=False,
    )
```

```python
import functools
import math

import jax
import jax.numpy as jnp
from jax import lax
from jax.experimental import pallas as pl
from jax.experimental.pallas import tpu as pltpu
from jax.sharding import PartitionSpec as P

epsilon = 1e-05
lanes = 128
turns = 4
plane = ("col", "chan")
whole = ("row", "col", "chan")
unit = 8


def kernel_params(mib):
    return pltpu.CompilerParams(vmem_limit_bytes=mib * 1024 * 1024)


def project_kernel(features, mask, left_weight, right_weight, left, right):
    depth, tokens = mask.shape
    width, inner = left_weight.shape
    group = lanes // width

    def chosen(rows, columns, test):
        a = lax.broadcasted_iota(jnp.int32, (rows, columns), 0)
        b = lax.broadcasted_iota(jnp.int32, (rows, columns), 1)
        return jnp.where(test(a, b), 1.0, 0.0).astype(jnp.bfloat16)

    dot = lambda a, b: jnp.dot(a, b, preferred_element_type=jnp.float32)
    repeat_rows = chosen(group * inner, inner, lambda a, b: a % inner == b)
    repeat_lanes = chosen(width, lanes, lambda a, b: a == b % width)
    own_block = chosen(group * inner, lanes, lambda a, b: a // inner == b // width)
    spread = []
    for weight in (left_weight, right_weight):
        tall = lax.dot_general(
            repeat_rows,
            weight[...],
            (((1,), (1,)), ((), ())),
            preferred_element_type=jnp.float32,
        ).astype(jnp.bfloat16)
        spread.append(dot(tall, repeat_lanes).astype(jnp.bfloat16) * own_block)
    both = jnp.concatenate(spread, axis=1)
    kept = mask[...].astype(jnp.float32).astype(jnp.bfloat16)
    wide_mask = dot(kept, chosen(tokens, tokens * width, lambda a, b: a == b // width))
    for g in range(tokens // group):
        at = slice(g * lanes, (g + 1) * lanes)
        value = dot(features[:, g * group * inner : (g + 1) * group * inner], both)
        left[:, at] = (value[:, :lanes] * wide_mask[:, at]).astype(jnp.bfloat16)
        right[:, at] = (value[:, lanes:] * wide_mask[:, at]).astype(jnp.bfloat16)
    narrow = dot(kept, chosen(tokens, lanes, lambda a, b: a == b)).astype(jnp.bfloat16)
    left[:, tokens * width :] = narrow
    right[:, tokens * width :] = narrow


def project_sides(features, mask, left_weight, right_weight):
    depth, tokens = mask.shape
    span = tokens * left_weight.shape[1] + lanes
    in_vmem = pl.BlockSpec(memory_space=pltpu.VMEM)
    return pl.pallas_call(
        project_kernel,
        in_specs=[in_vmem] * 4,
        out_specs=[in_vmem] * 2,
        out_shape=[jax.ShapeDtypeStruct((depth, span), jnp.bfloat16)] * 2,
        compiler_params=kernel_params(8),
        cost_estimate=pl.CostEstimate(flops=1024, bytes_accessed=1024, transcendentals=0),
    )(features.reshape(depth, -1), mask, left_weight.T, right_weight.T)


def arrange_kernel(
    places, *refs, row_blocks, col_blocks, width, tokens_row, tokens_col
):
    row_refs, refs = refs[:row_blocks], refs[row_blocks:]
    col_refs, refs = refs[:col_blocks], refs[col_blocks:]
    row_side, lane_side, scale, gathered, turned, row_mask, col_mask = refs
    high = width // turns
    row_span, col_span = tokens_row * width, tokens_col * width
    for n, block in enumerate(row_refs):
        at = pl.ds(pl.multiple_of(places[n], 16), block.shape[0])
        gathered[at, :] = block[:, :row_span]
        row_mask[at, :] = block[:, row_span:]
    for n, block in enumerate(col_refs):
        at = pl.ds(pl.multiple_of(places[row_blocks + n], 16), block.shape[0])
        col_mask[at, :] = block[:, col_span:]
        for g in range(col_span // lanes):
            spot = slice(g * lanes, (g + 1) * lanes)
            piece = block[:, spot]
            lane_side[0, at, spot] = piece
            piece = piece.astype(jnp.float32)
            for turn in range(1, turns):
                lane_side[turn, at, spot] = pltpu.roll(piece, turn * width, 1).astype(jnp.bfloat16)
    for n in range(row_span // lanes):
        spot = slice(n * lanes, (n + 1) * lanes)
        turned[spot, :] = gathered[:, spot].astype(jnp.float32).T
    for channel in range(width):
        spot = ((channel % turns) * high + channel // turns) * tokens_row
        rows = turned[pl.ds(channel, tokens_row, stride=width), :]
        row_side[spot : spot + tokens_row, :] = rows.astype(jnp.bfloat16)
    counts = lax.dot_general(
        row_mask[...],
        col_mask[...],
        (((0,), (0,)), ((), ())),
        preferred_element_type=jnp.float32,
    )[:tokens_row]
    inverse = 1.0 / jnp.maximum(counts, 1.0)
    strip = scale.shape[0]
    for n in range(strip):
        count = tokens_col // strip
        scale[n, :, :count] = inverse[:, n * count : (n + 1) * count]


def arrange(places, row_side, col_side, width, tokens_row, tokens_col):
    depth = sum(block.shape[0] for block in row_side)
    body = functools.partial(
        arrange_kernel,
        row_blocks=len(row_side),
        col_blocks=len(col_side),
        width=width,
        tokens_row=tokens_row,
        tokens_col=tokens_col,
    )
    in_vmem = pl.BlockSpec(memory_space=pltpu.VMEM)
    return pl.pallas_call(
        body,
        in_specs=[pl.BlockSpec(memory_space=pltpu.SMEM)]
        + [in_vmem] * (len(row_side) + len(col_side)),
        out_specs=[in_vmem] * 3,
        out_shape=[
            jax.ShapeDtypeStruct((tokens_row * width, depth), jnp.bfloat16),
            jax.ShapeDtypeStruct((turns, depth, tokens_col * width), jnp.bfloat16),
            jax.ShapeDtypeStruct((tokens_col // unit, tokens_row, lanes), jnp.float32),
        ],
        scratch_shapes=[
            pltpu.VMEM((depth, tokens_row * width), jnp.bfloat16),
            pltpu.VMEM((tokens_row * width, depth), jnp.float32),
            pltpu.VMEM((depth, lanes), jnp.bfloat16),
            pltpu.VMEM((depth, lanes), jnp.bfloat16),
        ],
        compiler_params=kernel_params(12),
        cost_estimate=pl.CostEstimate(flops=1024, bytes_accessed=1024, transcendentals=0),
    )(places, *row_side, *col_side)


def transition_rows(values, gate_up, down):
    channels = values.shape[1]
    mean_of = jnp.full((channels, channels), 1.0 / channels, jnp.bfloat16)
    centre = jnp.dot(values.astype(jnp.bfloat16), mean_of, preferred_element_type=jnp.float32)
    offset = values - centre
    squares = (offset * offset).astype(jnp.bfloat16)
    spread = jnp.dot(squares, mean_of, preferred_element_type=jnp.float32)
    normed = (offset * lax.rsqrt(spread + epsilon)).astype(jnp.bfloat16)
    both = jnp.dot(normed, gate_up, preferred_element_type=jnp.float32)
    hidden_width = gate_up.shape[1] // 2
    half, up = both[:, :hidden_width], both[:, hidden_width:]
    hidden = ((half + half * jnp.tanh(half)) * up).astype(jnp.bfloat16)
    return values + jnp.dot(hidden, down, preferred_element_type=jnp.float32)


def tile_kernel(
    row_side,
    lane_side,
    scale,
    base,
    weight,
    gate_up,
    down,
    out,
    products,
    stacked,
    held,
    *,
    first,
    width,
):
    strip, tokens_row, channels = out.shape
    high = width // turns
    groups = strip // turns
    span = high * tokens_row
    for turn in range(turns):
        products[turn] = jnp.dot(
            row_side[turn * span : (turn + 1) * span, :],
            lane_side[turn, :, first * width : (first + strip) * width],
            preferred_element_type=jnp.float32,
        ).astype(jnp.bfloat16)
    position = lax.broadcasted_iota(jnp.int32, (tokens_row, lanes), 1) // width
    for g in range(groups):
        for h in range(high):
            parts = [
                products[t, h * tokens_row : (h + 1) * tokens_row, g * lanes : (g + 1) * lanes]
                for t in range(turns)
            ]
            for u in range(turns):
                mixed = parts[(turns - 1 - u) % turns]
                for t in range(turns - 1):
                    mixed = jnp.where(position == t, parts[(t - u) % turns], mixed)
                stacked[
                    u, g * tokens_row : (g + 1) * tokens_row, h * lanes : (h + 1) * lanes
                ] = mixed
    for u in range(turns):
        update = jnp.dot(stacked[u], weight[u], preferred_element_type=jnp.float32)
        for g in range(groups):
            n = turns * g + u
            at = first + n
            factor = scale[at // unit][:, at % unit : at % unit + 1]
            value = update[g * tokens_row : (g + 1) * tokens_row] * factor
            value = base[at].astype(jnp.float32) + value
            held[n * tokens_row : (n + 1) * tokens_row, :] = value.astype(jnp.bfloat16)
    piece = strip if strip <= 32 else strip // 2
    for start in range(0, strip, piece):
        at = slice(start * tokens_row, (start + piece) * tokens_row)
        result = transition_rows(held[at, :].astype(jnp.float32), gate_up[...], down[...])
        out[start : start + piece] = result.astype(out.dtype).reshape(piece, tokens_row, channels)


def tile_strip(first, strip, row_side, lane_side, scale, base, weight, gate_up, down):
    tokens_row, channels = base.shape[1:]
    width = lane_side.shape[2] // base.shape[0]
    operands = [row_side, lane_side, scale, base, weight, gate_up, down]
    in_vmem = pl.BlockSpec(memory_space=pltpu.VMEM)
    return pl.pallas_call(
        functools.partial(tile_kernel, first=first, width=width),
        in_specs=[in_vmem] * len(operands),
        out_specs=in_vmem,
        out_shape=jax.ShapeDtypeStruct((strip, tokens_row, channels), jnp.bfloat16),
        scratch_shapes=[
            pltpu.VMEM((turns, tokens_row * width // turns, strip * width), jnp.bfloat16),
            pltpu.VMEM((turns, strip // turns * tokens_row, width * width), jnp.bfloat16),
            pltpu.VMEM((strip * tokens_row, channels), jnp.bfloat16),
        ],
        compiler_params=kernel_params(40),
        cost_estimate=pl.CostEstimate(flops=1024, bytes_accessed=1024, transcendentals=0),
    )(*operands)


def conv_kernel(
    valid_i, pair_two, *refs, parts
):
    counts = [len(p) for p in parts]
    total_parts = sum(counts)
    mirrored, refs = refs[:total_parts], refs[total_parts:]
    valid_j, top, bottom, left, right, weight, out, padded, centre = refs
    step = pl.program_id(0)
    rows, columns, channels = pair_two.shape
    strip = out.shape[0]

    @pl.when(step == 0)
    def _():
        padded[0, 8 : 8 + columns, :] = top[...].astype(jnp.float32)
        padded[rows + 1, 8 : 8 + columns, :] = bottom[...].astype(jnp.float32)
        i = 0
        used = 0
        for count in counts:
            group = mirrored[used : used + count]
            used += count
            for n in range(group[0].shape[0]):
                other = group[0][n].astype(jnp.float32)
                for more in group[1:]:
                    other = other + more[n].astype(jnp.float32)
                symmetric = (pair_two[i].astype(jnp.float32) + other) * 0.5
                centre[i] = symmetric
                keep = valid_j[...] * valid_i[i].astype(jnp.float32)
                padded[i + 1, 8 : 8 + columns, :] = symmetric * keep
                i += 1
        for i in range(rows + 2):
            padded[i, 7:8, :] = left[i : i + 1, :].astype(jnp.float32)
            padded[i, 8 + columns : 9 + columns, :] = right[i : i + 1, :].astype(jnp.float32)

    window = padded.at[pl.ds(step * strip, strip + 2)]
    shifted = [
        window[:, 7 + b : 7 + b + columns, :]
        .astype(jnp.bfloat16)
        .reshape((strip + 2) * columns, channels)
        for b in range(3)
    ]
    taps = jnp.dot(
        jnp.concatenate(shifted, axis=1), weight[...], preferred_element_type=jnp.float32
    ).reshape(strip + 2, columns, 3 * channels)
    total = centre[pl.ds(step * strip, strip)]
    for a in range(3):
        total = total + taps[a : a + strip, :, a * channels : (a + 1) * channels]
    out[...] = total.astype(out.dtype)


def convolve(pair_two, mirrored, valid_i, valid_j, halos, weight):
    rows, columns, channels = pair_two.shape
    strip = math.gcd(32, rows)
    operands = [pair_two, *[a for part in mirrored for a in part], valid_j, *halos, weight]
    fixed = lambda a: pl.BlockSpec(a.shape, lambda n, rank=a.ndim: (0,) * rank)
    return pl.pallas_call(
        functools.partial(conv_kernel, parts=[tuple(range(len(part))) for part in mirrored]),
        grid=(rows // strip,),
        in_specs=[pl.BlockSpec(memory_space=pltpu.SMEM)] + [fixed(a) for a in operands],
        out_specs=pl.BlockSpec((strip, columns, channels), lambda n: (n, 0, 0)),
        out_shape=jax.ShapeDtypeStruct(pair_two.shape, jnp.bfloat16),
        scratch_shapes=[
            pltpu.VMEM((rows + 2, columns + 16, channels), jnp.float32),
            pltpu.VMEM((rows, columns, channels), jnp.float32),
        ],
        compiler_params=kernel_params(40),
        cost_estimate=pl.CostEstimate(
            flops=18 * rows * columns * channels * channels,
            bytes_accessed=3 << 20,
            transcendentals=0,
        ),
    )(valid_i, *operands)


def shifts(size, step):
    return [(n, (n + step) % size) for n in range(size)]


def on_device(
    pair_input,
    alignment_features,
    alignment_mask,
    token_valid,
    left_weight,
    right_weight,
    output_weight,
    gate_weight,
    up_weight,
    down_weight,
    kernel_weight,
):
    rows_dev, cols_dev, channels = pair_input.shape
    local_rows, local_tokens, align_width = alignment_features.shape
    width = left_weight.shape[1]
    row_count, col_count = lax.axis_size("row"), lax.axis_size(plane)
    x_count, core_count = lax.axis_size("col"), lax.axis_size("chan")
    row_index, col_index = lax.axis_index("row"), lax.axis_index(plane)
    x_index, core_index = lax.axis_index("col"), lax.axis_index("chan")
    square = row_count == col_count
    tiles = [(r, c) for r in range(row_count) for c in range(col_count)]
    place_of = lambda r, c: r * col_count + c

    flat = alignment_features.reshape(local_rows * local_tokens, align_width)
    mask_rows = alignment_mask.astype(jnp.float32)

    def project(flat, weight):
        value = jnp.dot(flat, weight, preferred_element_type=jnp.float32)
        value = value.reshape(local_rows, local_tokens, width) * mask_rows[:, :, None]
        return value.astype(jnp.bfloat16)

    narrow_mask = alignment_mask.astype(jnp.bfloat16)

    def beside(side, mask):
        depth, tokens = mask.shape
        room = jnp.pad(mask, ((0, 0), (0, lanes - tokens % lanes)))
        return jnp.concatenate([side.reshape(depth, tokens * width), room], axis=1)

    if square:
        left_block, right_block = project_sides(
            alignment_features, alignment_mask, left_weight, right_weight
        )
        mirror_pairs = [(place_of(r, c), place_of(c, r)) for r, c in tiles]
        first = lax.ppermute(left_block, whole, mirror_pairs)
        col_side, col_places = [right_block], [row_index]
        held_back, _ = lax.optimization_barrier((right_block, first))
        for step in range(1, row_count):
            block = right_block if step in (1, row_count - 1) else held_back
            col_side.append(lax.ppermute(block, "row", shifts(row_count, -step)))
            col_places.append((row_index + step) % row_count)
        row_side, row_places = [first], [col_index]
        for step in range(1, x_count):
            row_side.append(lax.ppermute(first, "col", shifts(x_count, -step)))
            row_places.append(((x_index + step) % x_count) * core_count + core_index)
        for step in range(1, core_count):
            for n in range(x_count):
                row_side.append(lax.ppermute(row_side[n], "chan", shifts(core_count, -step)))
                row_places.append(
                    ((x_index + n) % x_count) * core_count + (core_index + step) % core_count
                )
        places = jnp.stack(row_places + col_places).astype(jnp.int32) * local_rows
    else:
        left_wide = lax.all_gather(project(flat, left_weight), plane, axis=1, tiled=True)
        mask_wide = lax.all_gather(narrow_mask, plane, axis=1, tiled=True)
        turn = lambda a: lax.all_to_all(a, "row", split_axis=1, concat_axis=0, tiled=True)
        gather = lambda a: lax.all_gather(a, "row", axis=0, tiled=True)
        row_side = [beside(turn(left_wide), turn(mask_wide))]
        col_side = [beside(gather(project(flat, right_weight)), gather(narrow_mask))]
        places = jnp.zeros((2,), jnp.int32)

    split = output_weight.reshape(width // turns, turns, width, channels)
    weight = jnp.stack(
        [jnp.roll(split, u, axis=1).reshape(width * width, channels) for u in range(turns)]
    )
    gate_up = jnp.concatenate([gate_weight * 0.5, up_weight], axis=1).astype(jnp.bfloat16)
    conv_weight = kernel_weight.transpose(1, 2, 0, 3).reshape(3 * channels, 3 * channels)
    base = jnp.swapaxes(pair_input, 0, 1)

    sides = arrange(places, row_side, col_side, width, rows_dev, cols_dev)

    def run(first, strip, after=None):
        row_channels = sides[0]
        if after is not None:
            row_channels, _ = lax.optimization_barrier((row_channels, after))
        return tile_strip(
            first, strip, row_channels, *sides[1:], base, weight, gate_up, down_weight
        )

    ahead = lambda size: [(n, n + 1) for n in range(size - 1)]
    back = lambda size: [(n + 1, n) for n in range(size - 1)]

    if square and cols_dev % (8 * unit) == 0 and x_count > 1:
        part = cols_dev // 16
        host = lambda r, c: place_of(r, (r // core_count) * core_count + c % core_count)
        away = [(r, c) for r, c in tiles if r // core_count != c // core_count]
        near = [(r, c) for r, c in tiles if r // core_count == c // core_count]
        to_host = [(place_of(r, c), host(r, c)) for r, c in away]
        from_host = [(host(r, c), place_of(c, r)) for r, c in away]
        beside_pairs = [(place_of(r, c), place_of(c, r)) for r, c in near]
        send = lambda value, pairs: lax.ppermute(value, whole, pairs)
        opening = run(0, 7 * part)
        hosted = send(opening, to_host)
        mirrored_near = send(opening, beside_pairs)
        rest = run(7 * part, 9 * part, opening)
        mirrored_rest = send(rest, mirror_pairs)
        mirrored_away = send(hosted, from_host)
        turned = jnp.concatenate([opening, rest], axis=0)
        mirrored = [[mirrored_away, mirrored_near], [mirrored_rest]]
    else:
        turned = run(0, cols_dev)
        share = rows_dev // col_count
        fold = row_count // col_count
        second = lax.all_to_all(
            lax.all_to_all(
                jnp.swapaxes(turned, 0, 1), plane, split_axis=0, concat_axis=1, tiled=True
            ),
            "row",
            split_axis=1,
            concat_axis=0,
            tiled=True,
        )
        third = lax.all_to_all(
            jnp.swapaxes(second, 0, 1), plane, split_axis=1, concat_axis=1, tiled=True
        )
        full = (
            third.reshape(rows_dev, col_count, fold, share, channels)
            .transpose(0, 2, 1, 3, 4)
            .reshape(rows_dev, cols_dev, channels)
        )
        mirrored = [[full]]

    pair_two = jnp.swapaxes(turned, 0, 1)
    valid_i = lax.dynamic_slice_in_dim(token_valid, row_index * rows_dev, rows_dev)
    valid_j = lax.dynamic_slice_in_dim(token_valid, col_index * cols_dev, cols_dev)
    keep_i = valid_i.astype(jnp.float32)[:, None]
    keep_j = valid_j.astype(jnp.float32)[:, None]
    last_i, last_j = rows_dev - 1, cols_dev - 1
    parts = [[a.astype(jnp.float32) for a in part] for part in mirrored]
    along = lambda pick: jnp.concatenate([sum(pick(a) for a in part) for part in parts], axis=0)

    def edge(own, other, keep):
        return ((own.astype(jnp.float32) + other) * 0.5 * keep).astype(jnp.bfloat16)

    first_line = edge(turned[:, 0], sum(a[0] for a in parts[0]), keep_j * keep_i[0])
    last_line = edge(turned[:, -1], sum(a[-1] for a in parts[-1]), keep_j * keep_i[last_i])
    first_side = edge(turned[0], along(lambda a: a[:, 0]), keep_i * keep_j[0])
    last_side = edge(turned[-1], along(lambda a: a[:, -1]), keep_i * keep_j[last_j])
    left = lax.ppermute(last_side, plane, ahead(col_count))
    right = lax.ppermute(first_side, plane, back(col_count))
    border = lambda i, line: jnp.concatenate([left[i][None], line, right[i][None]], axis=0)
    top = lax.ppermute(border(last_i, last_line), "row", ahead(row_count))
    bottom = lax.ppermute(border(0, first_line), "row", back(row_count))
    left = jnp.concatenate([top[:1], left, bottom[:1]], axis=0)
    right = jnp.concatenate([top[-1:], right, bottom[-1:]], axis=0)
    wide_valid = jnp.broadcast_to(keep_j, (cols_dev, channels))
    return convolve(
        pair_two,
        mirrored,
        valid_i,
        wide_valid,
        [top[1:-1], bottom[1:-1], left, right],
        conv_weight,
    )


def solution(mesh):
    placed = (
        P(("groups", "row"), plane, None),
        P("row", ("groups", "col", "chan"), None),
        P("row", ("groups", "col", "chan")),
        P("groups"),
        P(),
        P(),
        P(),
        P(),
        P(),
        P(),
        P(),
    )
    return jax.shard_map(
        on_device,
        mesh=mesh,
        in_specs=placed,
        out_specs=P(("groups", "row"), plane, None),
        check_vma=False,
    )
```
